512 devices in a mesh: seq: 8 (over x, core), chan: 64 (over z, y).
Axes of the slice: x: 4, y: 8, z: 8, core: 2. Of those that a mesh axis runs over, the one named last changes fastest.
Arguments:
- activations: bfloat16 [4096, 4096], P('seq', 'chan'), may hold values from -6 to 6
- in_weight: bfloat16 [3, 4096, 4096], P(None, 'chan'), may hold values from -0.09375 to 0.09375
- short_taps: float32 [3, 3, 4096], P(None, None, 'chan'), may hold values from -3.5 to 3.5
- long_filter: bfloat16 [4096, 4096], P('chan', 'seq'), may hold values from -0.09375 to 0.09375
- skip_gain: float32 [4096], P('chan'), may hold values from -4 to 4
Outputs:
- mixed: bfloat16 [4096, 4096], P('seq', 'chan')
The draws below stay inside these ranges and needn't reach their ends.
All inputs are finite; a program needn't handle non-finite values.
Results may differ from the reference program's by a relative error of at most 0.0076.
Values may be sent and summed in bfloat16 or wider, within the bound.
No kernel may reach another device: no remote copies, remote signals or barrier semaphores. Data moves between devices by JAX's collectives and lax.ppermute only.
A program may use at most 64 MiB of HBM per device.

```python
import math
import jax
import jax.numpy as jnp
from jax import lax

D = 4096
TOK_DEV = 512
TOKENS = 4096


def levels(key, dims, pieces, least, largest):
    def one(dim, shards_of):
        heights = jax.random.uniform(jax.random.fold_in(jax.random.fold_in(key, 6), dim), (shards_of,), jnp.float32, least / len(pieces), largest / len(pieces))
        return jnp.repeat(jnp.exp(heights), dims[dim] // shards_of).reshape((-1,) + (1,) * (len(dims) - dim - 1))

    loudness = one(*pieces[0])
    for cut in pieces[1:]:
        loudness = loudness * one(*cut)
    return loudness


def normal_values(key, extent, scale, most, pieces=(), held_as=jnp.bfloat16):
    values = scale * jax.random.normal(key, extent, jnp.float32)
    if pieces:
        values = values * levels(key, extent, pieces, -0.22, 0.18)
    return jnp.clip(values, -most, most).astype(held_as)


def setup_inputs(seed: int = 0) -> dict:
    seeds = jax.random.split(jax.random.key(seed), 6)
    activations = normal_values(seeds[0], (TOKENS, D), 1.0, 6.0, ((0, 8), (1, 64)))
    in_weight = normal_values(seeds[1], (3, D, D), D ** -0.5, 0.09375, ((1, 64),))
    short_taps = normal_values(seeds[2], (3, 3, D), 3 ** -0.5, 3.5, ((2, 64),), jnp.float32)
    long_filter = normal_values(seeds[3], (D, TOKENS), TOKENS ** -0.5, 0.09375, ((0, 64), (1, 8)))
    skip_gain = normal_values(seeds[4], (D,), 1.0, 4.0, ((0, 64),), jnp.float32)
    return {"activations": activations, "in_weight": in_weight, "short_taps": short_taps, "long_filter": long_filter, "skip_gain": skip_gain}


def tables(length):
    double = 2 * length
    freq_index = jnp.arange(double, dtype=jnp.int32)
    phase = ((freq_index[:, None] * freq_index[None, :]) % double).astype(jnp.float32) * (2.0 * math.pi / double)
    return jnp.cos(phase).astype(jnp.bfloat16), jnp.sin(phase).astype(jnp.bfloat16)


def reference(activations, in_weight, short_taps, long_filter, skip_gain):
    length = activations.shape[0]
    width = activations.shape[1]
    flat_weight = in_weight.reshape(3 * width, width)
    proj = jnp.dot(activations, flat_weight.T, preferred_element_type=jnp.float32).astype(jnp.bfloat16)
    proj = proj.reshape(length, 3, width).astype(jnp.float32)
    padded = jnp.concatenate([jnp.zeros((2, 3, width), jnp.float32), proj], axis=0)
    feat = short_taps[:, 0, :] * padded[2:] + short_taps[:, 1, :] * padded[1:-1] + short_taps[:, 2, :] * padded[:-2]
    gated = (feat[:, 1, :] * feat[:, 2, :]).astype(jnp.bfloat16)
    block = TOK_DEV
    count = length // block
    double = 2 * block
    cos_table, sin_table = tables(block)
    cos_fwd = cos_table[:, :block].astype(jnp.float32)
    sin_fwd = sin_table[:, :block].astype(jnp.float32)
    highest = lax.Precision.HIGHEST
    sig_blocks = gated.astype(jnp.float32).reshape(count, block, width)
    sig_re = jnp.einsum("ft,btc->bfc", cos_fwd, sig_blocks, precision=highest)
    sig_im = -jnp.einsum("ft,btc->bfc", sin_fwd, sig_blocks, precision=highest)
    fil_blocks = long_filter.astype(jnp.float32).reshape(width, count, block)
    fil_re = jnp.einsum("ft,cbt->bfc", cos_fwd, fil_blocks, precision=highest)
    fil_im = -jnp.einsum("ft,cbt->bfc", sin_fwd, fil_blocks, precision=highest)
    cos_inv = cos_table.astype(jnp.float32)
    sin_inv = sin_table.astype(jnp.float32)
    outputs = []
    for index in range(count):
        cur_re = jnp.zeros((double, width), jnp.float32)
        cur_im = jnp.zeros((double, width), jnp.float32)
        prev_re = jnp.zeros((double, width), jnp.float32)
        prev_im = jnp.zeros((double, width), jnp.float32)
        for source in range(index + 1):
            lag = index - source
            cur_re = cur_re + fil_re[lag] * sig_re[source] - fil_im[lag] * sig_im[source]
            cur_im = cur_im + fil_re[lag] * sig_im[source] + fil_im[lag] * sig_re[source]
            if lag >= 1:
                prev_re = prev_re + fil_re[lag - 1] * sig_re[source] - fil_im[lag - 1] * sig_im[source]
                prev_im = prev_im + fil_re[lag - 1] * sig_im[source] + fil_im[lag - 1] * sig_re[source]
        cur_re = cur_re.astype(jnp.bfloat16).astype(jnp.float32)
        cur_im = cur_im.astype(jnp.bfloat16).astype(jnp.float32)
        prev_re = prev_re.astype(jnp.bfloat16).astype(jnp.float32)
        prev_im = prev_im.astype(jnp.bfloat16).astype(jnp.float32)
        part = (jnp.dot(cos_inv[:block], cur_re, precision=highest)
                - jnp.dot(sin_inv[:block], cur_im, precision=highest)
                + jnp.dot(cos_inv[block:], prev_re, precision=highest)
                - jnp.dot(sin_inv[block:], prev_im, precision=highest)) / double
        outputs.append(part)
    conv = jnp.concatenate(outputs, axis=0)
    return (feat[:, 0, :] * (conv + skip_gain * gated.astype(jnp.float32))).astype(jnp.bfloat16)
```

```python
import math

import jax
import jax.numpy as jnp
import numpy as np
from jax import lax
from jax.experimental import pallas as pl
from jax.experimental.pallas import tpu as pltpu
from jax.sharding import PartitionSpec as P

BOTH = ("seq", "chan")
RING = 8
BLOCK = 512
F32 = jnp.float32
BF16 = jnp.bfloat16


def device_number(x, core, z, y):
    return ((x * 2 + core) * RING + z % RING) * RING + y % RING


def devices():
    return [
        (x, core, z, y)
        for x in range(4)
        for core in range(2)
        for z in range(RING)
        for y in range(RING)
    ]


def rings():
    return [
        [
            device_number(x, core, line, i) if core == 0 else device_number(x, core, i, line)
            for i in range(RING)
        ]
        for x in range(4)
        for core in range(2)
        for line in range(RING)
    ]


def shift(block, step):
    route = [
        (
            device_number(x, core, z, y),
            device_number(x, core, z + step, y)
            if core == 0
            else device_number(x, core, z, y + step),
        )
        for x, core, z, y in devices()
    ]
    return lax.ppermute(block, BOTH, route)


def tables():
    double = 2 * BLOCK
    freq = np.arange(BLOCK, dtype=np.int64)
    index = (freq[:, None] * freq[None, :]) % double
    phase = index.astype(np.float32) * np.float32(2.0 * math.pi / double)
    cosine = np.cos(phase).astype(jnp.bfloat16).astype(np.float32)
    sine = np.sin(phase).astype(jnp.bfloat16).astype(np.float32)
    nyquist = (1 - 2 * (freq % 2)).astype(np.float32)
    real, imag = cosine, -sine
    imag = imag.copy()
    imag[0] = nyquist
    forward = np.concatenate([real.T, imag.T], axis=1)
    weight = np.full((BLOCK, 1), 2.0 / double, np.float32)
    weight[0] = 1.0 / double
    inverse = np.concatenate([real * weight, imag * weight], axis=0)
    return forward.astype(jnp.bfloat16), inverse.astype(jnp.bfloat16)


def vmem():
    return pl.BlockSpec(memory_space=pltpu.VMEM)


def smem():
    return pl.BlockSpec(memory_space=pltpu.SMEM)


def params(mib):
    return pltpu.CompilerParams(vmem_limit_bytes=mib * 1024 * 1024)


def weight_kernel(place, weight, out):
    @pl.when(place[0] == 0)
    def _():
        for b in range(RING):
            out[b] = weight[:, b * BLOCK : (b + 1) * BLOCK]

    @pl.when(place[0] != 0)
    def _():
        for b in range(RING):
            out[b] = jnp.concatenate(
                [weight[:, (i * RING + b) * 64 : (i * RING + b) * 64 + 64] for i in range(RING)],
                axis=1,
            )


def first_kernel(place, weight, own, m1, p1, m2, p2, out):
    r = place[1]
    total = None
    for offset, block in ((0, own), (-1, m1), (1, p1), (-2, m2), (2, p2)):
        part = jnp.dot(
            weight[lax.rem(r + offset + RING, RING)], block[...], preferred_element_type=F32
        )
        total = part if total is None else total + part
    out[...] = total


def second_kernel(place, weight, before, m3, p3, low, high, lags, out):
    r = place[1]
    half = BLOCK // 2
    total = before[...]
    for offset, block in ((-3, m3), (3, p3)):
        total = total + jnp.dot(
            weight[lax.rem(r + offset + RING, RING)], block[...], preferred_element_type=F32
        )
    far = lax.rem(r + 4, RING)
    total = total + jnp.dot(weight[far, :, :half], low[...], preferred_element_type=F32)
    total = total + jnp.dot(weight[far, :, half:], high[...], preferred_element_type=F32)
    lag_rows = lags[...].astype(F32)
    pieces = []
    for d in range(RING):
        for s in range(3):
            pieces.append(total[s * 64 + d * 8 : s * 64 + d * 8 + 8])
        pieces.append(lag_rows[d * 8 : d * 8 + 8])
    out[...] = jnp.concatenate(pieces, axis=0).astype(BF16)


def conv_kernel(rows, taps, forward, inverse, out):
    data = rows[...].astype(F32)
    lane = lax.broadcasted_iota(jnp.int32, (8, RING * BLOCK), 1)

    def stream(s):
        return jnp.concatenate(
            [data[b * 32 + s * 8 : b * 32 + s * 8 + 8] for b in range(RING)], axis=1
        )

    def feature(s):
        now = stream(s)
        one = jnp.where(lane < 1, 0.0, pltpu.roll(now, 1, 1))
        two = jnp.where(lane < 2, 0.0, pltpu.roll(now, 2, 1))
        t = [taps[:, s * 3 + j : s * 3 + j + 1] for j in range(3)]
        return t[0] * now + t[1] * one + t[2] * two

    def by_block(value):
        return jnp.concatenate(
            [value[:, b * BLOCK : (b + 1) * BLOCK] for b in range(RING)], axis=0
        )

    gated = by_block(feature(1) * feature(2)).astype(BF16)
    lags = jnp.concatenate([data[b * 32 + 24 : b * 32 + 32] for b in range(RING)], axis=0)
    spec = jnp.dot(
        jnp.concatenate([gated, lags.astype(BF16)], axis=0),
        forward[...],
        preferred_element_type=F32,
    )
    reals, imags = [[] for _ in range(RING)], [[] for _ in range(RING)]
    wide = 128
    for piece in range(BLOCK // wide):
        here = slice(piece * wide, (piece + 1) * wide)
        there = slice(BLOCK + piece * wide, BLOCK + (piece + 1) * wide)
        freq = lax.broadcasted_iota(jnp.int32, (8, wide), 1) + piece * wide
        sign = (1 - 2 * lax.rem(freq, 2)).astype(F32)
        sig_re = [spec[b * 8 : b * 8 + 8, here] for b in range(RING)]
        sig_im = [spec[b * 8 : b * 8 + 8, there] for b in range(RING)]
        fil_re, fil_im, fil_last = [], [], []
        for m in range(RING):
            row = 64 + m * 8
            re, im = spec[row : row + 8, here], spec[row : row + 8, there]
            if m:
                re = re + sign * spec[row - 8 : row, here]
                im = im + sign * spec[row - 8 : row, there]
            fil_re.append(re)
            if piece == 0:
                fil_im.append(jnp.where(freq == 0, 0.0, im))
                fil_last.append(jnp.where(freq == 0, im, re))
            else:
                fil_im.append(im)
                fil_last.append(re)
        for b in range(RING):
            re = im = None
            for j in range(b + 1):
                m = b - j
                one = fil_re[m] * sig_re[j] - fil_im[m] * sig_im[j]
                two = fil_last[m] * sig_im[j] + fil_im[m] * sig_re[j]
                re = one if re is None else re + one
                im = two if im is None else im + two
            reals[b].append(re)
            imags[b].append(im)
    product = jnp.concatenate(
        [jnp.concatenate(reals[b] + imags[b], axis=1) for b in range(RING)], axis=0
    ).astype(BF16)
    conv = jnp.dot(product, inverse[...], preferred_element_type=F32)
    query = by_block(feature(0))
    skip = jnp.concatenate([taps[:, 9:10]] * RING, axis=0)
    out[...] = (query * (conv + skip * gated.astype(F32))).astype(BF16)


def on_device(activations, in_weight, short_taps, long_filter, skip_gain):
    position = lax.axis_index("seq")
    core = position % 2
    chan = lax.axis_index("chan")
    ring_place = jnp.where(core == 0, chan // RING, chan % RING)
    place = jnp.stack([core, ring_place]).astype(jnp.int32)

    shard = activations.T
    own = lax.all_to_all(
        jnp.broadcast_to(shard[None], (RING,) + shard.shape),
        BOTH,
        0,
        0,
        tiled=True,
        axis_index_groups=rings(),
    ).reshape(BLOCK, BLOCK)
    m2, p2 = shift(own, 2), shift(own, -2)
    m1, p1 = shift(own, 1), shift(own, -1)
    half = BLOCK // 2
    m3, p3 = shift(m2, 1), shift(p2, -1)
    low, high = shift(m2[:half], 2), shift(p2[half:], -2)

    weight = pl.pallas_call(
        weight_kernel,
        out_shape=jax.ShapeDtypeStruct((RING, 192, BLOCK), BF16),
        in_specs=[smem(), vmem()],
        out_specs=vmem(),
        compiler_params=params(24),
        cost_estimate=pl.CostEstimate(flops=0, bytes_accessed=3 << 20, transcendentals=0),
    )(place, in_weight.reshape(192, RING * BLOCK))
    before = pl.pallas_call(
        first_kernel,
        out_shape=jax.ShapeDtypeStruct((192, BLOCK), F32),
        in_specs=[smem()] + [vmem()] * 6,
        out_specs=vmem(),
        compiler_params=params(24),
        cost_estimate=pl.CostEstimate(
            flops=2 * 5 * 192 * BLOCK * BLOCK, bytes_accessed=4 << 20, transcendentals=0
        ),
    )(place, weight, own, m1, p1, m2, p2)
    messages = pl.pallas_call(
        second_kernel,
        out_shape=jax.ShapeDtypeStruct((RING * 32, BLOCK), BF16),
        in_specs=[smem()] + [vmem()] * 7,
        out_specs=vmem(),
        compiler_params=params(24),
        cost_estimate=pl.CostEstimate(
            flops=2 * 3 * 192 * BLOCK * BLOCK, bytes_accessed=4 << 20, transcendentals=0
        ),
    )(place, weight, before, m3, p3, low, high, long_filter)

    rows = lax.all_to_all(messages.reshape(RING, 32, BLOCK), "seq", 0, 0, tiled=True)
    taps = jnp.concatenate([short_taps.reshape(9, 64), skip_gain[None]], axis=0)
    taps = lax.dynamic_slice_in_dim(taps, position * 8, 8, axis=1).T
    forward, inverse = tables()
    mixed = pl.pallas_call(
        conv_kernel,
        out_shape=jax.ShapeDtypeStruct((RING * 8, BLOCK), BF16),
        in_specs=[vmem()] * 4,
        out_specs=vmem(),
        compiler_params=params(32),
        cost_estimate=pl.CostEstimate(
            flops=2 * (128 * 512 * 1024 + 64 * 1024 * 512), bytes_accessed=3 << 20, transcendentals=0
        ),
    )(rows.reshape(RING * 32, BLOCK), taps, forward, inverse)
    back = lax.all_to_all(mixed.reshape(RING, 8, BLOCK), "seq", 0, 0, tiled=True)
    return back.reshape(64, BLOCK).T


def solution(mesh):
    in_specs = (
        P("seq", "chan"),
        P(None, "chan", None),
        P(None, None, "chan"),
        P("chan", "seq"),
        P("chan"),
    )
    return jax.shard_map(
        on_device, mesh=mesh, in_specs=in_specs, out_specs=P("seq", "chan"), check_vma=False
    )
```

```python
import math

import jax
import jax.numpy as jnp
import numpy as np
from jax import lax
from jax.experimental import pallas as pl
from jax.experimental.pallas import tpu as pltpu
from jax.sharding import PartitionSpec as P

BOTH = ("seq", "chan")
RING = 8
BLOCK = 512
F32 = jnp.float32
BF16 = jnp.bfloat16


def device_number(x, core, z, y):
    return ((x * 2 + core) * RING + z % RING) * RING + y % RING


def devices():
    return [
        (x, core, z, y)
        for x in range(4)
        for core in range(2)
        for z in range(RING)
        for y in range(RING)
    ]


def rings():
    return [
        [
            device_number(x, core, line, i) if core == 0 else device_number(x, core, i, line)
            for i in range(RING)
        ]
        for x in range(4)
        for core in range(2)
        for line in range(RING)
    ]


def shift(block, even, odd):
    route = []
    for x, core, z, y in devices():
        here = y if core else z
        there = here + (odd if here % 2 else even)
        route.append(
            (
                device_number(x, core, z, y),
                device_number(x, core, z, there) if core else device_number(x, core, there, y),
            )
        )
    return lax.ppermute(block, BOTH, route)


def tables():
    double = 2 * BLOCK
    freq = np.arange(BLOCK, dtype=np.int64)
    index = (freq[:, None] * freq[None, :]) % double
    phase = index.astype(np.float32) * np.float32(2.0 * math.pi / double)
    cosine = np.cos(phase).astype(jnp.bfloat16).astype(np.float32)
    sine = np.sin(phase).astype(jnp.bfloat16).astype(np.float32)
    nyquist = (1 - 2 * (freq % 2)).astype(np.float32)
    real, imag = cosine, -sine
    imag = imag.copy()
    imag[0] = nyquist
    forward = np.concatenate([real.T, imag.T], axis=1)
    weight = np.full((BLOCK, 1), 2.0 / double, np.float32)
    weight[0] = 1.0 / double
    inverse = np.concatenate([real * weight, imag * weight], axis=0)
    return forward.astype(jnp.bfloat16), inverse.astype(jnp.bfloat16)


def vmem():
    return pl.BlockSpec(memory_space=pltpu.VMEM)


def smem():
    return pl.BlockSpec(memory_space=pltpu.SMEM)


def params(mib):
    return pltpu.CompilerParams(vmem_limit_bytes=mib * 1024 * 1024)


def weight_kernel(place, weight, out):
    @pl.when(place[0] == 0)
    def _():
        for b in range(RING):
            out[b] = weight[:, b * BLOCK : (b + 1) * BLOCK]

    @pl.when(place[0] != 0)
    def _():
        for b in range(RING):
            out[b] = jnp.concatenate(
                [weight[:, (i * RING + b) * 64 : (i * RING + b) * 64 + 64] for i in range(RING)],
                axis=1,
            )


def project(place, weight, blocks, total):
    r = place[1]
    sign = 1 - 2 * lax.rem(r, 2)
    for offset, block in blocks:
        part = jnp.dot(
            weight[lax.rem(r + sign * offset + RING, RING)],
            block[...],
            preferred_element_type=F32,
        )
        total = part if total is None else total + part
    return total


def first_kernel(place, weight, own, one_a, one_b, two_a, two_b, out):
    blocks = ((0, own), (1, one_a), (-1, one_b), (-2, two_a), (2, two_b))
    out[...] = project(place, weight, blocks, None)


def second_kernel(place, weight, before, four, three_a, three_b, lags, out):
    total = project(place, weight, ((4, four), (3, three_a), (-3, three_b)), before[...])
    lag_rows = lags[...].astype(F32)
    pieces = []
    for d in range(RING):
        for s in range(3):
            pieces.append(total[s * 64 + d * 8 : s * 64 + d * 8 + 8])
        pieces.append(lag_rows[d * 8 : d * 8 + 8])
    out[...] = jnp.concatenate(pieces, axis=0).astype(BF16)


def conv_kernel(rows, taps, forward, inverse, out):
    data = rows[...].astype(F32)
    lane = lax.broadcasted_iota(jnp.int32, (8, RING * BLOCK), 1)

    def stream(s):
        return jnp.concatenate(
            [data[b * 32 + s * 8 : b * 32 + s * 8 + 8] for b in range(RING)], axis=1
        )

    def feature(s):
        now = stream(s)
        one = jnp.where(lane < 1, 0.0, pltpu.roll(now, 1, 1))
        two = jnp.where(lane < 2, 0.0, pltpu.roll(now, 2, 1))
        t = [taps[:, s * 3 + j : s * 3 + j + 1] for j in range(3)]
        return t[0] * now + t[1] * one + t[2] * two

    def by_block(value):
        return jnp.concatenate(
            [value[:, b * BLOCK : (b + 1) * BLOCK] for b in range(RING)], axis=0
        )

    gated = by_block(feature(1) * feature(2)).astype(BF16)
    lags = jnp.concatenate([data[b * 32 + 24 : b * 32 + 32] for b in range(RING)], axis=0)
    spec = jnp.dot(
        jnp.concatenate([gated, lags.astype(BF16)], axis=0),
        forward[...],
        preferred_element_type=F32,
    )
    reals, imags = [[] for _ in range(RING)], [[] for _ in range(RING)]
    wide = 128
    for piece in range(BLOCK // wide):
        here = slice(piece * wide, (piece + 1) * wide)
        there = slice(BLOCK + piece * wide, BLOCK + (piece + 1) * wide)
        freq = lax.broadcasted_iota(jnp.int32, (8, wide), 1) + piece * wide
        sign = (1 - 2 * lax.rem(freq, 2)).astype(F32)
        sig_re = [spec[b * 8 : b * 8 + 8, here] for b in range(RING)]
        sig_im = [spec[b * 8 : b * 8 + 8, there] for b in range(RING)]
        fil_re, fil_im, fil_last = [], [], []
        for m in range(RING):
            row = 64 + m * 8
            re, im = spec[row : row + 8, here], spec[row : row + 8, there]
            if m:
                re = re + sign * spec[row - 8 : row, here]
                im = im + sign * spec[row - 8 : row, there]
            fil_re.append(re)
            if piece == 0:
                fil_im.append(jnp.where(freq == 0, 0.0, im))
                fil_last.append(jnp.where(freq == 0, im, re))
            else:
                fil_im.append(im)
                fil_last.append(re)
        for b in range(RING):
            re = im = None
            for j in range(b + 1):
                m = b - j
                one = fil_re[m] * sig_re[j] - fil_im[m] * sig_im[j]
                two = fil_last[m] * sig_im[j] + fil_im[m] * sig_re[j]
                re = one if re is None else re + one
                im = two if im is None else im + two
            reals[b].append(re)
            imags[b].append(im)
    product = jnp.concatenate(
        [jnp.concatenate(reals[b] + imags[b], axis=1) for b in range(RING)], axis=0
    ).astype(BF16)
    conv = jnp.dot(product, inverse[...], preferred_element_type=F32)
    query = by_block(feature(0))
    skip = jnp.concatenate([taps[:, 9:10]] * RING, axis=0)
    out[...] = (query * (conv + skip * gated.astype(F32))).astype(BF16)


def on_device(activations, in_weight, short_taps, long_filter, skip_gain):
    position = lax.axis_index("seq")
    core = position % 2
    chan = lax.axis_index("chan")
    ring_place = jnp.where(core == 0, chan // RING, chan % RING)
    place = jnp.stack([core, ring_place]).astype(jnp.int32)

    shard = activations.T
    own = lax.all_to_all(
        jnp.broadcast_to(shard[None], (RING,) + shard.shape),
        BOTH,
        0,
        0,
        tiled=True,
        axis_index_groups=rings(),
    ).reshape(BLOCK, BLOCK)
    two_a, two_b = shift(own, 2, -2), shift(own, -2, 2)
    one_a, one_b = shift(own, 1, -1), shift(own, -1, 1)
    four = shift(two_a, 2, -2)
    three_a, three_b = shift(two_a, 1, -1), shift(two_b, -1, 1)

    weight = pl.pallas_call(
        weight_kernel,
        out_shape=jax.ShapeDtypeStruct((RING, 192, BLOCK), BF16),
        in_specs=[smem(), vmem()],
        out_specs=vmem(),
        compiler_params=params(12),
        cost_estimate=pl.CostEstimate(flops=0, bytes_accessed=3 << 20, transcendentals=0),
    )(place, in_weight.reshape(192, RING * BLOCK))
    before = pl.pallas_call(
        first_kernel,
        out_shape=jax.ShapeDtypeStruct((192, BLOCK), F32),
        in_specs=[smem()] + [vmem()] * 6,
        out_specs=vmem(),
        compiler_params=params(12),
        cost_estimate=pl.CostEstimate(
            flops=2 * 5 * 192 * BLOCK * BLOCK, bytes_accessed=4 << 20, transcendentals=0
        ),
    )(place, weight, own, one_a, one_b, two_a, two_b)
    messages = pl.pallas_call(
        second_kernel,
        out_shape=jax.ShapeDtypeStruct((RING * 32, BLOCK), BF16),
        in_specs=[smem()] + [vmem()] * 6,
        out_specs=vmem(),
        compiler_params=params(12),
        cost_estimate=pl.CostEstimate(
            flops=2 * 3 * 192 * BLOCK * BLOCK, bytes_accessed=4 << 20, transcendentals=0
        ),
    )(place, weight, before, four, three_a, three_b, long_filter)

    rows = lax.all_to_all(messages.reshape(RING, 32, BLOCK), "seq", 0, 0, tiled=True)
    taps = jnp.concatenate([short_taps.reshape(9, 64), skip_gain[None]], axis=0)
    taps = lax.dynamic_slice_in_dim(taps, position * 8, 8, axis=1).T
    forward, inverse = tables()
    mixed = pl.pallas_call(
        conv_kernel,
        out_shape=jax.ShapeDtypeStruct((RING * 8, BLOCK), BF16),
        in_specs=[vmem()] * 4,
        out_specs=vmem(),
        compiler_params=params(12),
        cost_estimate=pl.CostEstimate(
            flops=2 * (128 * 512 * 1024 + 64 * 1024 * 512), bytes_accessed=3 << 20, transcendentals=0
        ),
    )(rows.reshape(RING * 32, BLOCK), taps, forward, inverse)
    back = lax.all_to_all(mixed.reshape(RING, 8, BLOCK), "seq", 0, 0, tiled=True)
    return back.reshape(64, BLOCK).T


def solution(mesh):
    in_specs = (
        P("seq", "chan"),
        P(None, "chan", None),
        P(None, None, "chan"),
        P("chan", "seq"),
        P("chan"),
    )
    return jax.shard_map(
        on_device, mesh=mesh, in_specs=in_specs, out_specs=P("seq", "chan"), check_vma=False
    )
```

```python
import math

import jax
import jax.numpy as jnp
import numpy as np
from jax import lax
from jax.experimental import pallas as pl
from jax.experimental.pallas import tpu as pltpu
from jax.sharding import PartitionSpec as P

BOTH = ("seq", "chan")
RING = 8
BLOCK = 512
F32 = jnp.float32
BF16 = jnp.bfloat16


def device_number(x, core, z, y):
    return ((x * 2 + core) * RING + z % RING) * RING + y % RING


def devices():
    return [
        (x, core, z, y)
        for x in range(4)
        for core in range(2)
        for z in range(RING)
        for y in range(RING)
    ]


def rings():
    return [
        [
            device_number(x, core, line, i) if core == 0 else device_number(x, core, i, line)
            for i in range(RING)
        ]
        for x in range(4)
        for core in range(2)
        for line in range(RING)
    ]


def shift(block, even, odd):
    route = []
    for x, core, z, y in devices():
        here = y if core else z
        there = here + (odd if here % 2 else even)
        route.append(
            (
                device_number(x, core, z, y),
                device_number(x, core, z, there) if core else device_number(x, core, there, y),
            )
        )
    return lax.ppermute(block, BOTH, route)


def tables():
    double = 2 * BLOCK
    freq = np.arange(BLOCK, dtype=np.int64)
    index = (freq[:, None] * freq[None, :]) % double
    phase = index.astype(np.float32) * np.float32(2.0 * math.pi / double)
    cosine = np.cos(phase).astype(jnp.bfloat16).astype(np.float32)
    sine = np.sin(phase).astype(jnp.bfloat16).astype(np.float32)
    nyquist = (1 - 2 * (freq % 2)).astype(np.float32)
    real, imag = cosine, -sine
    imag = imag.copy()
    imag[0] = nyquist
    forward = np.concatenate([real.T, imag.T], axis=1)
    weight = np.full((BLOCK, 1), 2.0 / double, np.float32)
    weight[0] = 1.0 / double
    inverse = np.concatenate([real * weight, imag * weight], axis=0)
    return forward.astype(jnp.bfloat16), inverse.astype(jnp.bfloat16)


def vmem():
    return pl.BlockSpec(memory_space=pltpu.VMEM)


def smem():
    return pl.BlockSpec(memory_space=pltpu.SMEM)


def params(mib):
    return pltpu.CompilerParams(vmem_limit_bytes=mib * 1024 * 1024)


def weight_kernel(place, weight, out):
    @pl.when(place[0] == 0)
    def _():
        for b in range(RING):
            out[b] = weight[:, b * BLOCK : (b + 1) * BLOCK]

    @pl.when(place[0] != 0)
    def _():
        for b in range(RING):
            out[b] = jnp.concatenate(
                [weight[:, (i * RING + b) * 64 : (i * RING + b) * 64 + 64] for i in range(RING)],
                axis=1,
            )


def project(place, weight, blocks, total):
    r = place[1]
    sign = 1 - 2 * lax.rem(r, 2)
    for offset, block in blocks:
        part = jnp.dot(
            weight[lax.rem(r + sign * offset + RING, RING)],
            block[...],
            preferred_element_type=F32,
        )
        total = part if total is None else total + part
    return total


def first_kernel(place, weight, own, one_a, one_b, two_a, two_b, out):
    blocks = ((0, own), (1, one_a), (-1, one_b), (-2, two_a), (2, two_b))
    out[...] = project(place, weight, blocks, None)


def second_kernel(place, weight, before, four, three_a, out):
    out[...] = project(place, weight, ((4, four), (3, three_a)), before[...])


def third_kernel(place, weight, before, three_b, lags, out):
    total = project(place, weight, ((-3, three_b),), before[...])
    lag_rows = lags[...].astype(F32)
    pieces = []
    for d in range(RING):
        for s in range(3):
            pieces.append(total[s * 64 + d * 8 : s * 64 + d * 8 + 8])
        pieces.append(lag_rows[d * 8 : d * 8 + 8])
    out[...] = jnp.concatenate(pieces, axis=0).astype(BF16)


def conv_kernel(rows, taps, forward, inverse, out):
    data = rows[...].astype(F32)
    lane = lax.broadcasted_iota(jnp.int32, (8, RING * BLOCK), 1)

    def stream(s):
        return jnp.concatenate(
            [data[b * 32 + s * 8 : b * 32 + s * 8 + 8] for b in range(RING)], axis=1
        )

    def feature(s):
        now = stream(s)
        one = jnp.where(lane < 1, 0.0, pltpu.roll(now, 1, 1))
        two = jnp.where(lane < 2, 0.0, pltpu.roll(now, 2, 1))
        t = [taps[:, s * 3 + j : s * 3 + j + 1] for j in range(3)]
        return t[0] * now + t[1] * one + t[2] * two

    def by_block(value):
        return jnp.concatenate(
            [value[:, b * BLOCK : (b + 1) * BLOCK] for b in range(RING)], axis=0
        )

    gated = by_block(feature(1) * feature(2)).astype(BF16)
    lags = jnp.concatenate([data[b * 32 + 24 : b * 32 + 32] for b in range(RING)], axis=0)
    spec = jnp.dot(
        jnp.concatenate([gated, lags.astype(BF16)], axis=0),
        forward[...],
        preferred_element_type=F32,
    )
    reals, imags = [[] for _ in range(RING)], [[] for _ in range(RING)]
    wide = 128
    for piece in range(BLOCK // wide):
        here = slice(piece * wide, (piece + 1) * wide)
        there = slice(BLOCK + piece * wide, BLOCK + (piece + 1) * wide)
        freq = lax.broadcasted_iota(jnp.int32, (8, wide), 1) + piece * wide
        sign = (1 - 2 * lax.rem(freq, 2)).astype(F32)
        sig_re = [spec[b * 8 : b * 8 + 8, here] for b in range(RING)]
        sig_im = [spec[b * 8 : b * 8 + 8, there] for b in range(RING)]
        fil_re, fil_im, fil_last = [], [], []
        for m in range(RING):
            row = 64 + m * 8
            re, im = spec[row : row + 8, here], spec[row : row + 8, there]
            if m:
                re = re + sign * spec[row - 8 : row, here]
                im = im + sign * spec[row - 8 : row, there]
            fil_re.append(re)
            if piece == 0:
                fil_im.append(jnp.where(freq == 0, 0.0, im))
                fil_last.append(jnp.where(freq == 0, im, re))
            else:
                fil_im.append(im)
                fil_last.append(re)
        for b in range(RING):
            re = im = None
            for j in range(b + 1):
                m = b - j
                one = fil_re[m] * sig_re[j] - fil_im[m] * sig_im[j]
                two = fil_last[m] * sig_im[j] + fil_im[m] * sig_re[j]
                re = one if re is None else re + one
                im = two if im is None else im + two
            reals[b].append(re)
            imags[b].append(im)
    product = jnp.concatenate(
        [jnp.concatenate(reals[b] + imags[b], axis=1) for b in range(RING)], axis=0
    ).astype(BF16)
    conv = jnp.dot(product, inverse[...], preferred_element_type=F32)
    query = by_block(feature(0))
    skip = jnp.concatenate([taps[:, 9:10]] * RING, axis=0)
    out[...] = (query * (conv + skip * gated.astype(F32))).astype(BF16)


def on_device(activations, in_weight, short_taps, long_filter, skip_gain):
    position = lax.axis_index("seq")
    core = position % 2
    chan = lax.axis_index("chan")
    ring_place = jnp.where(core == 0, chan // RING, chan % RING)
    place = jnp.stack([core, ring_place]).astype(jnp.int32)

    shard = activations.T
    own = lax.all_to_all(
        jnp.broadcast_to(shard[None], (RING,) + shard.shape),
        BOTH,
        0,
        0,
        tiled=True,
        axis_index_groups=rings(),
    ).reshape(BLOCK, BLOCK)
    two_a, two_b = shift(own, 2, -2), shift(own, -2, 2)
    one_a, one_b = shift(own, 1, -1), shift(own, -1, 1)
    four = shift(two_a, 2, -2)
    three_a, three_b = shift(two_a, 1, -1), shift(two_b, -1, 1)

    weight = pl.pallas_call(
        weight_kernel,
        out_shape=jax.ShapeDtypeStruct((RING, 192, BLOCK), BF16),
        in_specs=[smem(), vmem()],
        out_specs=vmem(),
        compiler_params=params(12),
        cost_estimate=pl.CostEstimate(flops=0, bytes_accessed=3 << 20, transcendentals=0),
    )(place, in_weight.reshape(192, RING * BLOCK))
    before = pl.pallas_call(
        first_kernel,
        out_shape=jax.ShapeDtypeStruct((192, BLOCK), F32),
        in_specs=[smem()] + [vmem()] * 6,
        out_specs=vmem(),
        compiler_params=params(12),
        cost_estimate=pl.CostEstimate(
            flops=2 * 5 * 192 * BLOCK * BLOCK, bytes_accessed=4 << 20, transcendentals=0
        ),
    )(place, weight, own, one_a, one_b, two_a, two_b)
    before = pl.pallas_call(
        second_kernel,
        out_shape=jax.ShapeDtypeStruct((192, BLOCK), F32),
        in_specs=[smem()] + [vmem()] * 4,
        out_specs=vmem(),
        compiler_params=params(12),
        cost_estimate=pl.CostEstimate(
            flops=2 * 2 * 192 * BLOCK * BLOCK, bytes_accessed=3 << 20, transcendentals=0
        ),
    )(place, weight, before, four, three_a)
    messages = pl.pallas_call(
        third_kernel,
        out_shape=jax.ShapeDtypeStruct((RING * 32, BLOCK), BF16),
        in_specs=[smem()] + [vmem()] * 4,
        out_specs=vmem(),
        compiler_params=params(12),
        cost_estimate=pl.CostEstimate(
            flops=2 * 192 * BLOCK * BLOCK, bytes_accessed=2 << 20, transcendentals=0
        ),
    )(place, weight, before, three_b, long_filter)

    rows = lax.all_to_all(messages.reshape(RING, 32, BLOCK), "seq", 0, 0, tiled=True)
    taps = jnp.concatenate([short_taps.reshape(9, 64), skip_gain[None]], axis=0)
    taps = lax.dynamic_slice_in_dim(taps, position * 8, 8, axis=1).T
    forward, inverse = tables()
    mixed = pl.pallas_call(
        conv_kernel,
        out_shape=jax.ShapeDtypeStruct((RING * 8, BLOCK), BF16),
        in_specs=[vmem()] * 4,
        out_specs=vmem(),
        compiler_params=params(12),
        cost_estimate=pl.CostEstimate(
            flops=2 * (128 * 512 * 1024 + 64 * 1024 * 512), bytes_accessed=3 << 20, transcendentals=0
        ),
    )(rows.reshape(RING * 32, BLOCK), taps, forward, inverse)
    back = lax.all_to_all(mixed.reshape(RING, 8, BLOCK), "seq", 0, 0, tiled=True)
    return back.reshape(64, BLOCK).T


def solution(mesh):
    in_specs = (
        P("seq", "chan"),
        P(None, "chan", None),
        P(None, None, "chan"),
        P("chan", "seq"),
        P("chan"),
    )
    return jax.shard_map(
        on_device, mesh=mesh, in_specs=in_specs, out_specs=P("seq", "chan"), check_vma=False
    )
```

```python
import math

import jax
import jax.numpy as jnp
import numpy as np
from jax import lax
from jax.experimental import pallas as pl
from jax.experimental.pallas import tpu as pltpu
from jax.sharding import PartitionSpec as P

BOTH = ("seq", "chan")
RING = 8
BLOCK = 512
F32 = jnp.float32
BF16 = jnp.bfloat16


def device_number(x, core, z, y):
    return ((x * 2 + core) * RING + z % RING) * RING + y % RING


def devices():
    return [
        (x, core, z, y)
        for x in range(4)
        for core in range(2)
        for z in range(RING)
        for y in range(RING)
    ]


def rings():
    return [
        [
            device_number(x, core, line, i) if core == 0 else device_number(x, core, i, line)
            for i in range(RING)
        ]
        for x in range(4)
        for core in range(2)
        for line in range(RING)
    ]


def shift(block, even, odd):
    route = []
    for x, core, z, y in devices():
        here = y if core else z
        there = here + (odd if here % 2 else even)
        route.append(
            (
                device_number(x, core, z, y),
                device_number(x, core, z, there) if core else device_number(x, core, there, y),
            )
        )
    return lax.ppermute(block, BOTH, route)


def tables():
    double = 2 * BLOCK
    freq = np.arange(BLOCK, dtype=np.int64)
    index = (freq[:, None] * freq[None, :]) % double
    phase = index.astype(np.float32) * np.float32(2.0 * math.pi / double)
    cosine = np.cos(phase).astype(jnp.bfloat16).astype(np.float32)
    sine = np.sin(phase).astype(jnp.bfloat16).astype(np.float32)
    nyquist = (1 - 2 * (freq % 2)).astype(np.float32)
    real, imag = cosine, -sine
    imag = imag.copy()
    imag[0] = nyquist
    forward = np.concatenate([real.T, imag.T], axis=1)
    weight = np.full((BLOCK, 1), 2.0 / double, np.float32)
    weight[0] = 1.0 / double
    inverse = np.concatenate([real * weight, imag * weight], axis=0)
    return forward.astype(jnp.bfloat16), inverse.astype(jnp.bfloat16)


def vmem():
    return pl.BlockSpec(memory_space=pltpu.VMEM)


def smem():
    return pl.BlockSpec(memory_space=pltpu.SMEM)


def params(mib):
    return pltpu.CompilerParams(vmem_limit_bytes=mib * 1024 * 1024)


def weight_kernel(place, weight, out):
    @pl.when(place[0] == 0)
    def _():
        for b in range(RING):
            out[b] = weight[:, b * BLOCK : (b + 1) * BLOCK]

    @pl.when(place[0] != 0)
    def _():
        for b in range(RING):
            out[b] = jnp.concatenate(
                [weight[:, (i * RING + b) * 64 : (i * RING + b) * 64 + 64] for i in range(RING)],
                axis=1,
            )


def project(place, weight, blocks, total):
    r = place[1]
    sign = 1 - 2 * lax.rem(r, 2)
    for offset, block in blocks:
        part = jnp.dot(
            weight[lax.rem(r + sign * offset + RING, RING)],
            block[...],
            preferred_element_type=F32,
        )
        total = part if total is None else total + part
    return total


def first_kernel(place, weight, own, one_a, one_b, two_a, two_b, out):
    blocks = ((0, own), (1, one_a), (-1, one_b), (-2, two_a), (2, two_b))
    out[...] = project(place, weight, blocks, None)


def second_kernel(place, weight, before, four, three_a, out):
    out[...] = project(place, weight, ((4, four), (3, three_a)), before[...])


def third_kernel(place, weight, before, three_b, lags, out):
    total = project(place, weight, ((-3, three_b),), before[...])
    lag_rows = lags[...].astype(F32)
    pieces = []
    for d in range(RING):
        for s in range(3):
            pieces.append(total[s * 64 + d * 8 : s * 64 + d * 8 + 8])
        pieces.append(lag_rows[d * 8 : d * 8 + 8])
    out[...] = jnp.concatenate(pieces, axis=0).astype(BF16)


def conv_kernel(rows, taps, forward, inverse, out):
    data = rows[...].astype(F32)
    lane = lax.broadcasted_iota(jnp.int32, (8, RING * BLOCK), 1)

    def stream(s):
        return jnp.concatenate(
            [data[b * 32 + s * 8 : b * 32 + s * 8 + 8] for b in range(RING)], axis=1
        )

    def feature(s):
        now = stream(s)
        one = jnp.where(lane < 1, 0.0, pltpu.roll(now, 1, 1))
        two = jnp.where(lane < 2, 0.0, pltpu.roll(now, 2, 1))
        t = [taps[:, s * 3 + j : s * 3 + j + 1] for j in range(3)]
        return t[0] * now + t[1] * one + t[2] * two

    def by_block(value):
        return jnp.concatenate(
            [value[:, b * BLOCK : (b + 1) * BLOCK] for b in range(RING)], axis=0
        )

    gated = by_block(feature(1) * feature(2)).astype(BF16)
    lags = jnp.concatenate([data[b * 32 + 24 : b * 32 + 32] for b in range(RING)], axis=0)
    spec = jnp.dot(
        jnp.concatenate([gated, lags.astype(BF16)], axis=0),
        forward[...],
        preferred_element_type=F32,
    )
    reals, imags = [[] for _ in range(RING)], [[] for _ in range(RING)]
    wide = 128
    for piece in range(BLOCK // wide):
        here = slice(piece * wide, (piece + 1) * wide)
        there = slice(BLOCK + piece * wide, BLOCK + (piece + 1) * wide)
        freq = lax.broadcasted_iota(jnp.int32, (8, wide), 1) + piece * wide
        sign = (1 - 2 * lax.rem(freq, 2)).astype(F32)
        sig_re = [spec[b * 8 : b * 8 + 8, here] for b in range(RING)]
        sig_im = [spec[b * 8 : b * 8 + 8, there] for b in range(RING)]
        fil_re, fil_im, fil_last = [], [], []
        for m in range(RING):
            row = 64 + m * 8
            re, im = spec[row : row + 8, here], spec[row : row + 8, there]
            if m:
                re = re + sign * spec[row - 8 : row, here]
                im = im + sign * spec[row - 8 : row, there]
            fil_re.append(re)
            if piece == 0:
                fil_im.append(jnp.where(freq == 0, 0.0, im))
                fil_last.append(jnp.where(freq == 0, im, re))
            else:
                fil_im.append(im)
                fil_last.append(re)
        for b in range(RING):
            re = im = None
            for j in range(b + 1):
                m = b - j
                one = fil_re[m] * sig_re[j] - fil_im[m] * sig_im[j]
                two = fil_last[m] * sig_im[j] + fil_im[m] * sig_re[j]
                re = one if re is None else re + one
                im = two if im is None else im + two
            reals[b].append(re)
            imags[b].append(im)
    product = jnp.concatenate(
        [jnp.concatenate(reals[b] + imags[b], axis=1) for b in range(RING)], axis=0
    ).astype(BF16)
    conv = jnp.dot(product, inverse[...], preferred_element_type=F32)
    query = by_block(feature(0))
    skip = jnp.concatenate([taps[:, 9:10]] * RING, axis=0)
    out[...] = (query * (conv + skip * gated.astype(F32))).astype(BF16)


def on_device(activations, in_weight, short_taps, long_filter, skip_gain):
    position = lax.axis_index("seq")
    core = position % 2
    chan = lax.axis_index("chan")
    ring_place = jnp.where(core == 0, chan // RING, chan % RING)
    place = jnp.stack([core, ring_place]).astype(jnp.int32)

    shard = activations.T
    own = lax.all_to_all(
        jnp.broadcast_to(shard[None], (RING,) + shard.shape),
        BOTH,
        0,
        0,
        tiled=True,
        axis_index_groups=rings(),
    ).reshape(BLOCK, BLOCK)
    two_a, two_b = shift(own, 2, -2), shift(own, -2, 2)
    one_a, one_b = shift(own, 1, -1), shift(own, -1, 1)
    four = shift(two_a, 2, -2)
    three_a, three_b = shift(two_a, 1, -1), shift(two_b, -1, 1)

    taps = jnp.concatenate([short_taps.reshape(9, 64), skip_gain[None]], axis=0)
    taps = lax.dynamic_slice_in_dim(taps, position * 8, 8, axis=1).T
    place, taps = lax.optimization_barrier((place, taps))

    weight = pl.pallas_call(
        weight_kernel,
        out_shape=jax.ShapeDtypeStruct((RING, 192, BLOCK), BF16),
        in_specs=[smem(), vmem()],
        out_specs=vmem(),
        compiler_params=params(12),
        cost_estimate=pl.CostEstimate(flops=0, bytes_accessed=3 << 20, transcendentals=0),
    )(place, in_weight.reshape(192, RING * BLOCK))
    before = pl.pallas_call(
        first_kernel,
        out_shape=jax.ShapeDtypeStruct((192, BLOCK), F32),
        in_specs=[smem()] + [vmem()] * 6,
        out_specs=vmem(),
        compiler_params=params(12),
        cost_estimate=pl.CostEstimate(
            flops=2 * 5 * 192 * BLOCK * BLOCK, bytes_accessed=4 << 20, transcendentals=0
        ),
    )(place, weight, own, one_a, one_b, two_a, two_b)
    before = pl.pallas_call(
        second_kernel,
        out_shape=jax.ShapeDtypeStruct((192, BLOCK), F32),
        in_specs=[smem()] + [vmem()] * 4,
        out_specs=vmem(),
        compiler_params=params(12),
        cost_estimate=pl.CostEstimate(
            flops=2 * 2 * 192 * BLOCK * BLOCK, bytes_accessed=3 << 20, transcendentals=0
        ),
    )(place, weight, before, four, three_a)
    messages = pl.pallas_call(
        third_kernel,
        out_shape=jax.ShapeDtypeStruct((RING * 32, BLOCK), BF16),
        in_specs=[smem()] + [vmem()] * 4,
        out_specs=vmem(),
        compiler_params=params(12),
        cost_estimate=pl.CostEstimate(
            flops=2 * 192 * BLOCK * BLOCK, bytes_accessed=2 << 20, transcendentals=0
        ),
    )(place, weight, before, three_b, long_filter)

    rows = lax.all_to_all(messages.reshape(RING, 32, BLOCK), "seq", 0, 0, tiled=True)
    forward, inverse = tables()
    mixed = pl.pallas_call(
        conv_kernel,
        out_shape=jax.ShapeDtypeStruct((RING * 8, BLOCK), BF16),
        in_specs=[vmem()] * 4,
        out_specs=vmem(),
        compiler_params=params(12),
        cost_estimate=pl.CostEstimate(
            flops=2 * (128 * 512 * 1024 + 64 * 1024 * 512), bytes_accessed=3 << 20, transcendentals=0
        ),
    )(rows.reshape(RING * 32, BLOCK), taps, forward, inverse)
    back = lax.all_to_all(mixed.reshape(RING, 8, BLOCK), "seq", 0, 0, tiled=True)
    return back.reshape(64, BLOCK).T


def solution(mesh):
    in_specs = (
        P("seq", "chan"),
        P(None, "chan", None),
        P(None, None, "chan"),
        P("chan", "seq"),
        P("chan"),
    )
    return jax.shard_map(
        on_device, mesh=mesh, in_specs=in_specs, out_specs=P("seq", "chan"), check_vma=False
    )
```

```python
import math

import jax
import jax.numpy as jnp
import numpy as np
from jax import lax
from jax.experimental import pallas as pl
from jax.experimental.pallas import tpu as pltpu
from jax.sharding import PartitionSpec as P

BOTH = ("seq", "chan")
RING = 8
BLOCK = 512
F32 = jnp.float32
BF16 = jnp.bfloat16


def device_number(x, core, z, y):
    return ((x * 2 + core) * RING + z % RING) * RING + y % RING


def devices():
    return [
        (x, core, z, y)
        for x in range(4)
        for core in range(2)
        for z in range(RING)
        for y in range(RING)
    ]


def rings():
    return [
        [
            device_number(x, core, line, i) if core == 1 else device_number(x, core, i, line)
            for i in range(RING)
        ]
        for x in range(4)
        for core in range(2)
        for line in range(RING)
    ]


def shift(block, even, odd):
    route = []
    for x, core, z, y in devices():
        here = z if core else y
        there = here + (odd if here % 2 else even)
        route.append(
            (
                device_number(x, core, z, y),
                device_number(x, core, there, y) if core else device_number(x, core, z, there),
            )
        )
    return lax.ppermute(block, BOTH, route)


def tables():
    double = 2 * BLOCK
    freq = np.arange(BLOCK, dtype=np.int64)
    index = (freq[:, None] * freq[None, :]) % double
    phase = index.astype(np.float32) * np.float32(2.0 * math.pi / double)
    cosine = np.cos(phase).astype(jnp.bfloat16).astype(np.float32)
    sine = np.sin(phase).astype(jnp.bfloat16).astype(np.float32)
    nyquist = (1 - 2 * (freq % 2)).astype(np.float32)
    real, imag = cosine, -sine
    imag = imag.copy()
    imag[0] = nyquist
    forward = np.concatenate([real.T, imag.T], axis=1)
    weight = np.full((BLOCK, 1), 2.0 / double, np.float32)
    weight[0] = 1.0 / double
    inverse = np.concatenate([real * weight, imag * weight], axis=0)
    return forward.astype(jnp.bfloat16), inverse.astype(jnp.bfloat16)


def vmem():
    return pl.BlockSpec(memory_space=pltpu.VMEM)


def smem():
    return pl.BlockSpec(memory_space=pltpu.SMEM)


def anywhere():
    return pl.BlockSpec(memory_space=pl.ANY)


def landing(count):
    return [pltpu.VMEM((count, BLOCK, BLOCK), BF16), pltpu.SemaphoreType.DMA((count,))]


def params(mib):
    return pltpu.CompilerParams(vmem_limit_bytes=mib * 1024 * 1024)


def weight_kernel(place, weight, out):
    @pl.when(place[0] == 0)
    def _():
        for b in range(RING):
            out[b] = weight[:, b * BLOCK : (b + 1) * BLOCK]

    @pl.when(place[0] != 0)
    def _():
        for b in range(RING):
            out[b] = jnp.concatenate(
                [weight[:, (i * RING + b) * 64 : (i * RING + b) * 64 + 64] for i in range(RING)],
                axis=1,
            )


def project(place, weight, offsets, blocks, near, done, total):
    r = place[1]
    sign = 1 - 2 * lax.rem(r, 2)
    copies = [
        pltpu.make_async_copy(block, near.at[i], done.at[i]) for i, block in enumerate(blocks)
    ]
    for copy in copies:
        copy.start()
    for i, offset in enumerate(offsets):
        copies[i].wait()
        part = jnp.dot(
            weight[lax.rem(r + sign * offset + RING, RING)],
            near[i],
            preferred_element_type=F32,
        )
        total = part if total is None else total + part
    return total


def first_kernel(place, weight, own, one_a, one_b, two_a, two_b, four, out, near, done):
    blocks = (own, one_a, one_b, two_a, two_b, four)
    out[...] = project(place, weight, (0, 1, -1, -2, 2, 4), blocks, near, done, None)


def second_kernel(place, weight, before, three_a, three_b, lags, out, near, done):
    total = project(place, weight, (3, -3), (three_a, three_b), near, done, before[...])
    lag_rows = lags[...].astype(F32)
    pieces = []
    for d in range(RING):
        for s in range(3):
            pieces.append(total[s * 64 + d * 8 : s * 64 + d * 8 + 8])
        pieces.append(lag_rows[d * 8 : d * 8 + 8])
    out[...] = jnp.concatenate(pieces, axis=0).astype(BF16)


def conv_kernel(rows, taps, forward, inverse, out):
    data = rows[...].astype(F32)
    lane = lax.broadcasted_iota(jnp.int32, (8, RING * BLOCK), 1)

    def stream(s):
        return jnp.concatenate(
            [data[b * 32 + s * 8 : b * 32 + s * 8 + 8] for b in range(RING)], axis=1
        )

    def feature(s):
        now = stream(s)
        one = jnp.where(lane < 1, 0.0, pltpu.roll(now, 1, 1))
        two = jnp.where(lane < 2, 0.0, pltpu.roll(now, 2, 1))
        t = [taps[:, s * 3 + j : s * 3 + j + 1] for j in range(3)]
        return t[0] * now + t[1] * one + t[2] * two

    def by_block(value):
        return jnp.concatenate(
            [value[:, b * BLOCK : (b + 1) * BLOCK] for b in range(RING)], axis=0
        )

    gated = by_block(feature(1) * feature(2)).astype(BF16)
    lags = jnp.concatenate([data[b * 32 + 24 : b * 32 + 32] for b in range(RING)], axis=0)
    spec = jnp.dot(
        jnp.concatenate([gated, lags.astype(BF16)], axis=0),
        forward[...],
        preferred_element_type=F32,
    )
    reals, imags = [[] for _ in range(RING)], [[] for _ in range(RING)]
    wide = 128
    for piece in range(BLOCK // wide):
        here = slice(piece * wide, (piece + 1) * wide)
        there = slice(BLOCK + piece * wide, BLOCK + (piece + 1) * wide)
        freq = lax.broadcasted_iota(jnp.int32, (8, wide), 1) + piece * wide
        sign = (1 - 2 * lax.rem(freq, 2)).astype(F32)
        sig_re = [spec[b * 8 : b * 8 + 8, here] for b in range(RING)]
        sig_im = [spec[b * 8 : b * 8 + 8, there] for b in range(RING)]
        fil_re, fil_im, fil_last = [], [], []
        for m in range(RING):
            row = 64 + m * 8
            re, im = spec[row : row + 8, here], spec[row : row + 8, there]
            if m:
                re = re + sign * spec[row - 8 : row, here]
                im = im + sign * spec[row - 8 : row, there]
            fil_re.append(re)
            if piece == 0:
                fil_im.append(jnp.where(freq == 0, 0.0, im))
                fil_last.append(jnp.where(freq == 0, im, re))
            else:
                fil_im.append(im)
                fil_last.append(re)
        for b in range(RING):
            re = im = None
            for j in range(b + 1):
                m = b - j
                one = fil_re[m] * sig_re[j] - fil_im[m] * sig_im[j]
                two = fil_last[m] * sig_im[j] + fil_im[m] * sig_re[j]
                re = one if re is None else re + one
                im = two if im is None else im + two
            reals[b].append(re)
            imags[b].append(im)
    product = jnp.concatenate(
        [jnp.concatenate(reals[b] + imags[b], axis=1) for b in range(RING)], axis=0
    ).astype(BF16)
    conv = jnp.dot(product, inverse[...], preferred_element_type=F32)
    query = by_block(feature(0))
    skip = jnp.concatenate([taps[:, 9:10]] * RING, axis=0)
    out[...] = (query * (conv + skip * gated.astype(F32))).astype(BF16)


def on_device(activations, in_weight, short_taps, long_filter, skip_gain):
    position = lax.axis_index("seq")
    mixed_blocks = 1 - position % 2
    chan = lax.axis_index("chan")
    ring_place = jnp.where(mixed_blocks == 0, chan // RING, chan % RING)
    place = jnp.stack([mixed_blocks, ring_place]).astype(jnp.int32)

    shard = activations.T
    own = lax.all_to_all(
        jnp.broadcast_to(shard[None], (RING,) + shard.shape),
        BOTH,
        0,
        0,
        tiled=True,
        axis_index_groups=rings(),
    ).reshape(BLOCK, BLOCK)
    two_a, two_b = shift(own, 2, -2), shift(own, -2, 2)
    one_a, one_b = shift(own, 1, -1), shift(own, -1, 1)
    four = shift(two_a, 2, -2)
    three_a, three_b = shift(two_a, 1, -1), shift(two_b, -1, 1)

    taps = jnp.concatenate([short_taps.reshape(9, 64), skip_gain[None]], axis=0)
    taps = lax.dynamic_slice_in_dim(taps, position * 8, 8, axis=1).T
    place, taps = lax.optimization_barrier((place, taps))

    weight = pl.pallas_call(
        weight_kernel,
        out_shape=jax.ShapeDtypeStruct((RING, 192, BLOCK), BF16),
        in_specs=[smem(), vmem()],
        out_specs=vmem(),
        compiler_params=params(12),
        cost_estimate=pl.CostEstimate(flops=0, bytes_accessed=3 << 20, transcendentals=0),
    )(place, in_weight.reshape(192, RING * BLOCK))
    before = pl.pallas_call(
        first_kernel,
        out_shape=jax.ShapeDtypeStruct((192, BLOCK), F32),
        in_specs=[smem(), vmem()] + [anywhere()] * 6,
        out_specs=vmem(),
        scratch_shapes=landing(6),
        compiler_params=params(12),
        cost_estimate=pl.CostEstimate(
            flops=2 * 6 * 192 * BLOCK * BLOCK, bytes_accessed=5 << 20, transcendentals=0
        ),
    )(place, weight, own, one_a, one_b, two_a, two_b, four)
    messages = pl.pallas_call(
        second_kernel,
        out_shape=jax.ShapeDtypeStruct((RING * 32, BLOCK), BF16),
        in_specs=[smem(), vmem(), vmem()] + [anywhere()] * 2 + [vmem()],
        out_specs=vmem(),
        scratch_shapes=landing(2),
        compiler_params=params(12),
        cost_estimate=pl.CostEstimate(
            flops=2 * 2 * 192 * BLOCK * BLOCK, bytes_accessed=3 << 20, transcendentals=0
        ),
    )(place, weight, before, three_a, three_b, long_filter)

    rows = lax.all_to_all(messages.reshape(RING, 32, BLOCK), "seq", 0, 0, tiled=True)
    forward, inverse = tables()
    mixed = pl.pallas_call(
        conv_kernel,
        out_shape=jax.ShapeDtypeStruct((RING * 8, BLOCK), BF16),
        in_specs=[vmem()] * 4,
        out_specs=vmem(),
        compiler_params=params(12),
        cost_estimate=pl.CostEstimate(
            flops=2 * (128 * 512 * 1024 + 64 * 1024 * 512), bytes_accessed=3 << 20, transcendentals=0
        ),
    )(rows.reshape(RING * 32, BLOCK), taps, forward, inverse)
    back = lax.all_to_all(mixed.reshape(RING, 8, BLOCK), "seq", 0, 0, tiled=True)
    return back.reshape(64, BLOCK).T


def solution(mesh):
    in_specs = (
        P("seq", "chan"),
        P(None, "chan", None),
        P(None, None, "chan"),
        P("chan", "seq"),
        P("chan"),
    )
    return jax.shard_map(
        on_device, mesh=mesh, in_specs=in_specs, out_specs=P("seq", "chan"), check_vma=False
    )
```

```python
import math

import jax
import jax.numpy as jnp
import numpy as np
from jax import lax
from jax.experimental import pallas as pl
from jax.experimental.pallas import tpu as pltpu
from jax.sharding import PartitionSpec as P

BOTH = ("seq", "chan")
RING = 8
BLOCK = 512
F32 = jnp.float32
BF16 = jnp.bfloat16


def device_number(x, core, z, y):
    return ((x * 2 + core) * RING + z % RING) * RING + y % RING


def devices():
    return [
        (x, core, z, y)
        for x in range(4)
        for core in range(2)
        for z in range(RING)
        for y in range(RING)
    ]


def rings():
    return [
        [
            device_number(x, core, line, i) if core == 1 else device_number(x, core, i, line)
            for i in range(RING)
        ]
        for x in range(4)
        for core in range(2)
        for line in range(RING)
    ]


def shift(block, even, odd):
    route = []
    for x, core, z, y in devices():
        here = z if core else y
        there = here + (odd if (here + 1 - core) % 2 else even)
        route.append(
            (
                device_number(x, core, z, y),
                device_number(x, core, there, y) if core else device_number(x, core, z, there),
            )
        )
    return lax.ppermute(block, BOTH, route)


def tables():
    double = 2 * BLOCK
    freq = np.arange(BLOCK, dtype=np.int64)
    index = (freq[:, None] * freq[None, :]) % double
    phase = index.astype(np.float32) * np.float32(2.0 * math.pi / double)
    cosine = np.cos(phase).astype(jnp.bfloat16).astype(np.float32)
    sine = np.sin(phase).astype(jnp.bfloat16).astype(np.float32)
    nyquist = (1 - 2 * (freq % 2)).astype(np.float32)
    real, imag = cosine, -sine
    imag = imag.copy()
    imag[0] = nyquist
    forward = np.concatenate([real.T, imag.T], axis=1)
    weight = np.full((BLOCK, 1), 2.0 / double, np.float32)
    weight[0] = 1.0 / double
    inverse = np.concatenate([real * weight, imag * weight], axis=0)
    return forward.astype(jnp.bfloat16), inverse.astype(jnp.bfloat16)


def vmem():
    return pl.BlockSpec(memory_space=pltpu.VMEM)


def smem():
    return pl.BlockSpec(memory_space=pltpu.SMEM)


def anywhere():
    return pl.BlockSpec(memory_space=pl.ANY)


def landing(count):
    return [pltpu.VMEM((count, BLOCK, BLOCK), BF16), pltpu.SemaphoreType.DMA((count,))]


def params(mib):
    return pltpu.CompilerParams(vmem_limit_bytes=mib * 1024 * 1024)


def weight_kernel(place, weight, out):
    @pl.when(place[0] == 0)
    def _():
        for b in range(RING):
            out[b] = weight[:, b * BLOCK : (b + 1) * BLOCK]

    @pl.when(place[0] != 0)
    def _():
        for b in range(RING):
            out[b] = jnp.concatenate(
                [weight[:, (i * RING + b) * 64 : (i * RING + b) * 64 + 64] for i in range(RING)],
                axis=1,
            )


def project(place, weight, offsets, blocks, near, done, total):
    r = place[1]
    sign = 1 - 2 * lax.rem(r + place[0], 2)
    copies = [
        pltpu.make_async_copy(block, near.at[i], done.at[i]) for i, block in enumerate(blocks)
    ]
    for copy in copies:
        copy.start()
    for i, offset in enumerate(offsets):
        copies[i].wait()
        part = jnp.dot(
            weight[lax.rem(r + sign * offset + RING, RING)],
            near[i],
            preferred_element_type=F32,
        )
        total = part if total is None else total + part
    return total


def first_kernel(place, weight, own, one_a, one_b, two_a, two_b, four, out, near, done):
    blocks = (own, one_a, one_b, two_a, two_b, four)
    out[...] = project(place, weight, (0, 1, -1, -2, 2, 4), blocks, near, done, None)


def second_kernel(place, weight, before, three_a, three_b, lags, out, near, done):
    total = project(place, weight, (3, -3), (three_a, three_b), near, done, before[...])
    lag_rows = lags[...].astype(F32)
    pieces = []
    for d in range(RING):
        for s in range(3):
            pieces.append(total[s * 64 + d * 8 : s * 64 + d * 8 + 8])
        pieces.append(lag_rows[d * 8 : d * 8 + 8])
    out[...] = jnp.concatenate(pieces, axis=0).astype(BF16)


def conv_kernel(rows, taps, forward, inverse, out):
    data = rows[...].astype(F32)
    lane = lax.broadcasted_iota(jnp.int32, (8, RING * BLOCK), 1)

    def stream(s):
        return jnp.concatenate(
            [data[b * 32 + s * 8 : b * 32 + s * 8 + 8] for b in range(RING)], axis=1
        )

    def feature(s):
        now = stream(s)
        one = jnp.where(lane < 1, 0.0, pltpu.roll(now, 1, 1))
        two = jnp.where(lane < 2, 0.0, pltpu.roll(now, 2, 1))
        t = [taps[:, s * 3 + j : s * 3 + j + 1] for j in range(3)]
        return t[0] * now + t[1] * one + t[2] * two

    def by_block(value):
        return jnp.concatenate(
            [value[:, b * BLOCK : (b + 1) * BLOCK] for b in range(RING)], axis=0
        )

    gated = by_block(feature(1) * feature(2)).astype(BF16)
    lags = jnp.concatenate([data[b * 32 + 24 : b * 32 + 32] for b in range(RING)], axis=0)
    spec = jnp.dot(
        jnp.concatenate([gated, lags.astype(BF16)], axis=0),
        forward[...],
        preferred_element_type=F32,
    )
    reals, imags = [[] for _ in range(RING)], [[] for _ in range(RING)]
    wide = 128
    for piece in range(BLOCK // wide):
        here = slice(piece * wide, (piece + 1) * wide)
        there = slice(BLOCK + piece * wide, BLOCK + (piece + 1) * wide)
        freq = lax.broadcasted_iota(jnp.int32, (8, wide), 1) + piece * wide
        sign = (1 - 2 * lax.rem(freq, 2)).astype(F32)
        sig_re = [spec[b * 8 : b * 8 + 8, here] for b in range(RING)]
        sig_im = [spec[b * 8 : b * 8 + 8, there] for b in range(RING)]
        fil_re, fil_im, fil_last = [], [], []
        for m in range(RING):
            row = 64 + m * 8
            re, im = spec[row : row + 8, here], spec[row : row + 8, there]
            if m:
                re = re + sign * spec[row - 8 : row, here]
                im = im + sign * spec[row - 8 : row, there]
            fil_re.append(re)
            if piece == 0:
                fil_im.append(jnp.where(freq == 0, 0.0, im))
                fil_last.append(jnp.where(freq == 0, im, re))
            else:
                fil_im.append(im)
                fil_last.append(re)
        for b in range(RING):
            re = im = None
            for j in range(b + 1):
                m = b - j
                one = fil_re[m] * sig_re[j] - fil_im[m] * sig_im[j]
                two = fil_last[m] * sig_im[j] + fil_im[m] * sig_re[j]
                re = one if re is None else re + one
                im = two if im is None else im + two
            reals[b].append(re)
            imags[b].append(im)
    product = jnp.concatenate(
        [jnp.concatenate(reals[b] + imags[b], axis=1) for b in range(RING)], axis=0
    ).astype(BF16)
    conv = jnp.dot(product, inverse[...], preferred_element_type=F32)
    query = by_block(feature(0))
    skip = jnp.concatenate([taps[:, 9:10]] * RING, axis=0)
    out[...] = (query * (conv + skip * gated.astype(F32))).astype(BF16)


def on_device(activations, in_weight, short_taps, long_filter, skip_gain):
    position = lax.axis_index("seq")
    mixed_blocks = 1 - position % 2
    chan = lax.axis_index("chan")
    ring_place = jnp.where(mixed_blocks == 0, chan // RING, chan % RING)
    place = jnp.stack([mixed_blocks, ring_place]).astype(jnp.int32)

    shard = activations.T
    own = lax.all_to_all(
        jnp.broadcast_to(shard[None], (RING,) + shard.shape),
        BOTH,
        0,
        0,
        tiled=True,
        axis_index_groups=rings(),
    ).reshape(BLOCK, BLOCK)
    two_a, two_b = shift(own, 2, -2), shift(own, -2, 2)
    one_a, one_b = shift(own, 1, -1), shift(own, -1, 1)
    four = shift(two_a, 2, -2)
    three_a, three_b = shift(two_a, 1, -1), shift(two_b, -1, 1)

    taps = jnp.concatenate([short_taps.reshape(9, 64), skip_gain[None]], axis=0)
    taps = lax.dynamic_slice_in_dim(taps, position * 8, 8, axis=1).T
    place, taps = lax.optimization_barrier((place, taps))

    weight = pl.pallas_call(
        weight_kernel,
        out_shape=jax.ShapeDtypeStruct((RING, 192, BLOCK), BF16),
        in_specs=[smem(), vmem()],
        out_specs=vmem(),
        compiler_params=params(12),
        cost_estimate=pl.CostEstimate(flops=0, bytes_accessed=3 << 20, transcendentals=0),
    )(place, in_weight.reshape(192, RING * BLOCK))
    before = pl.pallas_call(
        first_kernel,
        out_shape=jax.ShapeDtypeStruct((192, BLOCK), F32),
        in_specs=[smem(), vmem()] + [anywhere()] * 6,
        out_specs=vmem(),
        scratch_shapes=landing(6),
        compiler_params=params(12),
        cost_estimate=pl.CostEstimate(
            flops=2 * 6 * 192 * BLOCK * BLOCK, bytes_accessed=5 << 20, transcendentals=0
        ),
    )(place, weight, own, one_a, one_b, two_a, two_b, four)
    messages = pl.pallas_call(
        second_kernel,
        out_shape=jax.ShapeDtypeStruct((RING * 32, BLOCK), BF16),
        in_specs=[smem(), vmem(), vmem()] + [anywhere()] * 2 + [vmem()],
        out_specs=vmem(),
        scratch_shapes=landing(2),
        compiler_params=params(12),
        cost_estimate=pl.CostEstimate(
            flops=2 * 2 * 192 * BLOCK * BLOCK, bytes_accessed=3 << 20, transcendentals=0
        ),
    )(place, weight, before, three_a, three_b, long_filter)

    rows = lax.all_to_all(messages.reshape(RING, 32, BLOCK), "seq", 0, 0, tiled=True)
    forward, inverse = tables()
    mixed = pl.pallas_call(
        conv_kernel,
        out_shape=jax.ShapeDtypeStruct((RING * 8, BLOCK), BF16),
        in_specs=[vmem()] * 4,
        out_specs=vmem(),
        compiler_params=params(12),
        cost_estimate=pl.CostEstimate(
            flops=2 * (128 * 512 * 1024 + 64 * 1024 * 512), bytes_accessed=3 << 20, transcendentals=0
        ),
    )(rows.reshape(RING * 32, BLOCK), taps, forward, inverse)
    back = lax.all_to_all(mixed.reshape(RING, 8, BLOCK), "seq", 0, 0, tiled=True)
    return back.reshape(64, BLOCK).T


def solution(mesh):
    in_specs = (
        P("seq", "chan"),
        P(None, "chan", None),
        P(None, None, "chan"),
        P("chan", "seq"),
        P("chan"),
    )
    return jax.shard_map(
        on_device, mesh=mesh, in_specs=in_specs, out_specs=P("seq", "chan"), check_vma=False
    )
```

```python
import math

import jax
import jax.numpy as jnp
import numpy as np
from jax import lax
from jax.experimental import pallas as pl
from jax.experimental.pallas import tpu as pltpu
from jax.sharding import PartitionSpec as P

BOTH = ("seq", "chan")
RING = 8
BLOCK = 512
F32 = jnp.float32
BF16 = jnp.bfloat16


def device_number(x, core, z, y):
    return ((x * 2 + core) * RING + z % RING) * RING + y % RING


def devices():
    return [
        (x, core, z, y)
        for x in range(4)
        for core in range(2)
        for z in range(RING)
        for y in range(RING)
    ]


def rings():
    return [
        [
            device_number(x, core, line, i) if core == 1 else device_number(x, core, i, line)
            for i in range(RING)
        ]
        for x in range(4)
        for core in range(2)
        for line in range(RING)
    ]


def shift(block, even, odd):
    route = []
    for x, core, z, y in devices():
        here = z if core else y
        there = here + (odd if (here + 1 - core) % 2 else even)
        route.append(
            (
                device_number(x, core, z, y),
                device_number(x, core, there, y) if core else device_number(x, core, z, there),
            )
        )
    return lax.ppermute(block, BOTH, route)


def tables():
    double = 2 * BLOCK
    freq = np.arange(BLOCK, dtype=np.int64)
    index = (freq[:, None] * freq[None, :]) % double
    phase = index.astype(np.float32) * np.float32(2.0 * math.pi / double)
    cosine = np.cos(phase).astype(jnp.bfloat16).astype(np.float32)
    sine = np.sin(phase).astype(jnp.bfloat16).astype(np.float32)
    nyquist = (1 - 2 * (freq % 2)).astype(np.float32)
    real, imag = cosine, -sine
    imag = imag.copy()
    imag[0] = nyquist
    forward = np.concatenate([real.T, imag.T], axis=1)
    weight = np.full((BLOCK, 1), 2.0 / double, np.float32)
    weight[0] = 1.0 / double
    inverse = np.concatenate([real * weight, imag * weight], axis=0)
    return forward.astype(jnp.bfloat16), inverse.astype(jnp.bfloat16)


def vmem():
    return pl.BlockSpec(memory_space=pltpu.VMEM)


def smem():
    return pl.BlockSpec(memory_space=pltpu.SMEM)


def anywhere():
    return pl.BlockSpec(memory_space=pl.ANY)


def landing(count):
    return [pltpu.VMEM((count, BLOCK, BLOCK), BF16), pltpu.SemaphoreType.DMA((count,))]


def params(mib):
    return pltpu.CompilerParams(vmem_limit_bytes=mib * 1024 * 1024)


def weight_kernel(place, weight, out):
    @pl.when(place[0] == 0)
    def _():
        for b in range(RING):
            out[b] = weight[:, b * BLOCK : (b + 1) * BLOCK]

    @pl.when(place[0] != 0)
    def _():
        for b in range(RING):
            out[b] = jnp.concatenate(
                [weight[:, (i * RING + b) * 64 : (i * RING + b) * 64 + 64] for i in range(RING)],
                axis=1,
            )


def project(place, weight, offsets, blocks, near, done, total):
    r = place[1]
    sign = 1 - 2 * lax.rem(r + place[0], 2)
    copies = [
        pltpu.make_async_copy(block, near.at[i], done.at[i]) for i, block in enumerate(blocks)
    ]
    for copy in copies:
        copy.start()
    for i, offset in enumerate(offsets):
        copies[i].wait()
        part = jnp.dot(
            weight[lax.rem(r + sign * offset + RING, RING)],
            near[i],
            preferred_element_type=F32,
        )
        total = part if total is None else total + part
    return total


def first_kernel(place, weight, own, one_a, one_b, two_a, two_b, four, out, near, done):
    blocks = (own, one_a, one_b, two_a, two_b, four)
    out[...] = project(place, weight, (0, 1, -1, -2, 2, 4), blocks, near, done, None)


def second_kernel(place, weight, before, three_a, three_b, lags, out, near, done):
    total = project(place, weight, (3, -3), (three_a, three_b), near, done, before[...])
    lag_rows = lags[...].astype(F32)
    pieces = []
    for d in range(RING):
        for s in range(3):
            pieces.append(total[s * 64 + d * 8 : s * 64 + d * 8 + 8])
        pieces.append(lag_rows[d * 8 : d * 8 + 8])
    out[...] = jnp.concatenate(pieces, axis=0).astype(BF16)


def conv_kernel(rows, taps, forward, inverse, out):
    data = rows[...].astype(F32)
    lane = lax.broadcasted_iota(jnp.int32, (8, RING * BLOCK), 1)

    def stream(s):
        return jnp.concatenate(
            [data[b * 32 + s * 8 : b * 32 + s * 8 + 8] for b in range(RING)], axis=1
        )

    def feature(s):
        now = stream(s)
        one = jnp.where(lane < 1, 0.0, pltpu.roll(now, 1, 1))
        two = jnp.where(lane < 2, 0.0, pltpu.roll(now, 2, 1))
        t = [taps[:, s * 3 + j : s * 3 + j + 1] for j in range(3)]
        return t[0] * now + t[1] * one + t[2] * two

    def by_block(value):
        return jnp.concatenate(
            [value[:, b * BLOCK : (b + 1) * BLOCK] for b in range(RING)], axis=0
        )

    gated = by_block(feature(1) * feature(2)).astype(BF16)
    lags = jnp.concatenate([data[b * 32 + 24 : b * 32 + 32] for b in range(RING)], axis=0)
    spec = jnp.dot(
        jnp.concatenate([gated, lags.astype(BF16)], axis=0),
        forward[...],
        preferred_element_type=F32,
    )
    reals, imags = [[] for _ in range(RING)], [[] for _ in range(RING)]
    wide = 128
    for piece in range(BLOCK // wide):
        here = slice(piece * wide, (piece + 1) * wide)
        there = slice(BLOCK + piece * wide, BLOCK + (piece + 1) * wide)
        freq = lax.broadcasted_iota(jnp.int32, (8, wide), 1) + piece * wide
        sign = (1 - 2 * lax.rem(freq, 2)).astype(F32)
        sig_re = [spec[b * 8 : b * 8 + 8, here] for b in range(RING)]
        sig_im = [spec[b * 8 : b * 8 + 8, there] for b in range(RING)]
        fil_re, fil_im, fil_last = [], [], []
        for m in range(RING):
            row = 64 + m * 8
            re, im = spec[row : row + 8, here], spec[row : row + 8, there]
            if m:
                re = re + sign * spec[row - 8 : row, here]
                im = im + sign * spec[row - 8 : row, there]
            fil_re.append(re)
            if piece == 0:
                fil_im.append(jnp.where(freq == 0, 0.0, im))
                fil_last.append(jnp.where(freq == 0, im, re))
            else:
                fil_im.append(im)
                fil_last.append(re)
        for b in range(RING):
            re = im = None
            for j in range(b + 1):
                m = b - j
                one = fil_re[m] * sig_re[j] - fil_im[m] * sig_im[j]
                two = fil_last[m] * sig_im[j] + fil_im[m] * sig_re[j]
                re = one if re is None else re + one
                im = two if im is None else im + two
            reals[b].append(re)
            imags[b].append(im)
    product = jnp.concatenate(
        [jnp.concatenate(reals[b] + imags[b], axis=1) for b in range(RING)], axis=0
    ).astype(BF16)
    conv = jnp.dot(product, inverse[...], preferred_element_type=F32)
    query = by_block(feature(0))
    skip = jnp.concatenate([taps[:, 9:10]] * RING, axis=0)
    out[...] = (query * (conv + skip * gated.astype(F32))).astype(BF16)


def on_device(activations, in_weight, short_taps, long_filter, skip_gain):
    position = lax.axis_index("seq")
    mixed_blocks = 1 - position % 2
    chan = lax.axis_index("chan")
    ring_place = jnp.where(mixed_blocks == 0, chan // RING, chan % RING)
    place = jnp.stack([mixed_blocks, ring_place]).astype(jnp.int32)

    shard = activations.T
    own = lax.all_to_all(
        jnp.broadcast_to(shard[None], (RING,) + shard.shape),
        BOTH,
        0,
        0,
        tiled=True,
        axis_index_groups=rings(),
    ).reshape(BLOCK, BLOCK)
    taps = jnp.concatenate([short_taps.reshape(9, 64), skip_gain[None]], axis=0)
    taps = lax.dynamic_slice_in_dim(taps, position * 8, 8, axis=1).T
    place, taps = lax.optimization_barrier((place, taps))

    weight = pl.pallas_call(
        weight_kernel,
        out_shape=jax.ShapeDtypeStruct((RING, 192, BLOCK), BF16),
        in_specs=[smem(), vmem()],
        out_specs=vmem(),
        compiler_params=params(12),
        cost_estimate=pl.CostEstimate(flops=0, bytes_accessed=3 << 20, transcendentals=0),
    )(place, in_weight.reshape(192, RING * BLOCK))
    two_a, two_b = shift(own, 2, -2), shift(own, -2, 2)
    later, weight = lax.optimization_barrier((own, weight))
    one_a, one_b = shift(later, 1, -1), shift(later, -1, 1)
    four = shift(two_a, 2, -2)
    three_a, three_b = shift(two_a, 1, -1), shift(two_b, -1, 1)

    before = pl.pallas_call(
        first_kernel,
        out_shape=jax.ShapeDtypeStruct((192, BLOCK), F32),
        in_specs=[smem(), vmem()] + [anywhere()] * 6,
        out_specs=vmem(),
        scratch_shapes=landing(6),
        compiler_params=params(12),
        cost_estimate=pl.CostEstimate(
            flops=2 * 6 * 192 * BLOCK * BLOCK, bytes_accessed=5 << 20, transcendentals=0
        ),
    )(place, weight, own, one_a, one_b, two_a, two_b, four)
    messages = pl.pallas_call(
        second_kernel,
        out_shape=jax.ShapeDtypeStruct((RING * 32, BLOCK), BF16),
        in_specs=[smem(), vmem(), vmem()] + [anywhere()] * 2 + [vmem()],
        out_specs=vmem(),
        scratch_shapes=landing(2),
        compiler_params=params(12),
        cost_estimate=pl.CostEstimate(
            flops=2 * 2 * 192 * BLOCK * BLOCK, bytes_accessed=3 << 20, transcendentals=0
        ),
    )(place, weight, before, three_a, three_b, long_filter)

    rows = lax.all_to_all(messages.reshape(RING, 32, BLOCK), "seq", 0, 0, tiled=True)
    forward, inverse = tables()
    mixed = pl.pallas_call(
        conv_kernel,
        out_shape=jax.ShapeDtypeStruct((RING * 8, BLOCK), BF16),
        in_specs=[vmem()] * 4,
        out_specs=vmem(),
        compiler_params=params(12),
        cost_estimate=pl.CostEstimate(
            flops=2 * (128 * 512 * 1024 + 64 * 1024 * 512), bytes_accessed=3 << 20, transcendentals=0
        ),
    )(rows.reshape(RING * 32, BLOCK), taps, forward, inverse)
    back = lax.all_to_all(mixed.reshape(RING, 8, BLOCK), "seq", 0, 0, tiled=True)
    return back.reshape(64, BLOCK).T


def solution(mesh):
    in_specs = (
        P("seq", "chan"),
        P(None, "chan", None),
        P(None, None, "chan"),
        P("chan", "seq"),
        P("chan"),
    )
    return jax.shard_map(
        on_device, mesh=mesh, in_specs=in_specs, out_specs=P("seq", "chan"), check_vma=False
    )
```

```python
import math

import jax
import jax.numpy as jnp
import numpy as np
from jax import lax
from jax.experimental import pallas as pl
from jax.experimental.pallas import tpu as pltpu
from jax.sharding import PartitionSpec as P

BOTH = ("seq", "chan")
RING = 8
BLOCK = 512
F32 = jnp.float32
BF16 = jnp.bfloat16


def device_number(x, core, z, y):
    return ((x * 2 + core) * RING + z % RING) * RING + y % RING


def devices():
    return [
        (x, core, z, y)
        for x in range(4)
        for core in range(2)
        for z in range(RING)
        for y in range(RING)
    ]


def rings():
    return [
        [
            device_number(x, core, line, i) if core == 1 else device_number(x, core, i, line)
            for i in range(RING)
        ]
        for x in range(4)
        for core in range(2)
        for line in range(RING)
    ]


def shift(block, even, odd):
    route = []
    for x, core, z, y in devices():
        here = z if core else y
        there = here + (odd if (here + 1 - core) % 2 else even)
        route.append(
            (
                device_number(x, core, z, y),
                device_number(x, core, there, y) if core else device_number(x, core, z, there),
            )
        )
    return lax.ppermute(block, BOTH, route)


def tables():
    double = 2 * BLOCK
    freq = np.arange(BLOCK, dtype=np.int64)
    index = (freq[:, None] * freq[None, :]) % double
    phase = index.astype(np.float32) * np.float32(2.0 * math.pi / double)
    cosine = np.cos(phase).astype(jnp.bfloat16).astype(np.float32)
    sine = np.sin(phase).astype(jnp.bfloat16).astype(np.float32)
    nyquist = (1 - 2 * (freq % 2)).astype(np.float32)
    real, imag = cosine, -sine
    imag = imag.copy()
    imag[0] = nyquist
    forward = np.concatenate([real.T, imag.T], axis=1)
    weight = np.full((BLOCK, 1), 2.0 / double, np.float32)
    weight[0] = 1.0 / double
    inverse = np.concatenate([real * weight, imag * weight], axis=0)
    return forward.astype(jnp.bfloat16), inverse.astype(jnp.bfloat16)


def vmem():
    return pl.BlockSpec(memory_space=pltpu.VMEM)


def smem():
    return pl.BlockSpec(memory_space=pltpu.SMEM)


def anywhere():
    return pl.BlockSpec(memory_space=pl.ANY)


def landing(count):
    return [pltpu.VMEM((count, BLOCK, BLOCK), BF16), pltpu.SemaphoreType.DMA((count,))]


def params(mib):
    return pltpu.CompilerParams(vmem_limit_bytes=mib * 1024 * 1024)


def weight_kernel(place, weight, out):
    @pl.when(place[0] == 0)
    def _():
        for b in range(RING):
            out[b] = weight[:, b * BLOCK : (b + 1) * BLOCK]

    @pl.when(place[0] != 0)
    def _():
        for b in range(RING):
            out[b] = jnp.concatenate(
                [weight[:, (i * RING + b) * 64 : (i * RING + b) * 64 + 64] for i in range(RING)],
                axis=1,
            )


def project(place, weight, offsets, blocks, near, done, total):
    r = place[1]
    sign = 1 - 2 * lax.rem(r + place[0], 2)
    copies = [
        pltpu.make_async_copy(block, near.at[i], done.at[i]) for i, block in enumerate(blocks)
    ]
    for copy in copies:
        copy.start()
    for i, offset in enumerate(offsets):
        copies[i].wait()
        part = jnp.dot(
            weight[lax.rem(r + sign * offset + RING, RING)],
            near[i],
            preferred_element_type=F32,
        )
        total = part if total is None else total + part
    return total


def own_kernel(place, weight, own, out, near, done):
    out[...] = project(place, weight, (0,), (own,), near, done, None)


def first_kernel(place, weight, before, one_a, one_b, two_a, two_b, four, out, near, done):
    blocks = (one_a, one_b, two_a, two_b, four)
    out[...] = project(place, weight, (1, -1, -2, 2, 4), blocks, near, done, before[...])


def second_kernel(place, weight, before, three_a, three_b, lags, out, near, done):
    total = project(place, weight, (3, -3), (three_a, three_b), near, done, before[...])
    lag_rows = lags[...].astype(F32)
    pieces = []
    for d in range(RING):
        for s in range(3):
            pieces.append(total[s * 64 + d * 8 : s * 64 + d * 8 + 8])
        pieces.append(lag_rows[d * 8 : d * 8 + 8])
    out[...] = jnp.concatenate(pieces, axis=0).astype(BF16)


def conv_kernel(rows, taps, forward, inverse, out):
    data = rows[...].astype(F32)
    lane = lax.broadcasted_iota(jnp.int32, (8, RING * BLOCK), 1)

    def stream(s):
        return jnp.concatenate(
            [data[b * 32 + s * 8 : b * 32 + s * 8 + 8] for b in range(RING)], axis=1
        )

    def feature(s):
        now = stream(s)
        one = jnp.where(lane < 1, 0.0, pltpu.roll(now, 1, 1))
        two = jnp.where(lane < 2, 0.0, pltpu.roll(now, 2, 1))
        t = [taps[:, s * 3 + j : s * 3 + j + 1] for j in range(3)]
        return t[0] * now + t[1] * one + t[2] * two

    def by_block(value):
        return jnp.concatenate(
            [value[:, b * BLOCK : (b + 1) * BLOCK] for b in range(RING)], axis=0
        )

    gated = by_block(feature(1) * feature(2)).astype(BF16)
    lags = jnp.concatenate([data[b * 32 + 24 : b * 32 + 32] for b in range(RING)], axis=0)
    spec = jnp.dot(
        jnp.concatenate([gated, lags.astype(BF16)], axis=0),
        forward[...],
        preferred_element_type=F32,
    )
    reals, imags = [[] for _ in range(RING)], [[] for _ in range(RING)]
    wide = 128
    for piece in range(BLOCK // wide):
        here = slice(piece * wide, (piece + 1) * wide)
        there = slice(BLOCK + piece * wide, BLOCK + (piece + 1) * wide)
        freq = lax.broadcasted_iota(jnp.int32, (8, wide), 1) + piece * wide
        sign = (1 - 2 * lax.rem(freq, 2)).astype(F32)
        sig_re = [spec[b * 8 : b * 8 + 8, here] for b in range(RING)]
        sig_im = [spec[b * 8 : b * 8 + 8, there] for b in range(RING)]
        fil_re, fil_im, fil_last = [], [], []
        for m in range(RING):
            row = 64 + m * 8
            re, im = spec[row : row + 8, here], spec[row : row + 8, there]
            if m:
                re = re + sign * spec[row - 8 : row, here]
                im = im + sign * spec[row - 8 : row, there]
            fil_re.append(re)
            if piece == 0:
                fil_im.append(jnp.where(freq == 0, 0.0, im))
                fil_last.append(jnp.where(freq == 0, im, re))
            else:
                fil_im.append(im)
                fil_last.append(re)
        for b in range(RING):
            re = im = None
            for j in range(b + 1):
                m = b - j
                one = fil_re[m] * sig_re[j] - fil_im[m] * sig_im[j]
                two = fil_last[m] * sig_im[j] + fil_im[m] * sig_re[j]
                re = one if re is None else re + one
                im = two if im is None else im + two
            reals[b].append(re)
            imags[b].append(im)
    product = jnp.concatenate(
        [jnp.concatenate(reals[b] + imags[b], axis=1) for b in range(RING)], axis=0
    ).astype(BF16)
    conv = jnp.dot(product, inverse[...], preferred_element_type=F32)
    query = by_block(feature(0))
    skip = jnp.concatenate([taps[:, 9:10]] * RING, axis=0)
    out[...] = (query * (conv + skip * gated.astype(F32))).astype(BF16)


def on_device(activations, in_weight, short_taps, long_filter, skip_gain):
    position = lax.axis_index("seq")
    mixed_blocks = 1 - position % 2
    chan = lax.axis_index("chan")
    ring_place = jnp.where(mixed_blocks == 0, chan // RING, chan % RING)
    place = jnp.stack([mixed_blocks, ring_place]).astype(jnp.int32)

    shard = activations.T
    own = lax.all_to_all(
        jnp.broadcast_to(shard[None], (RING,) + shard.shape),
        BOTH,
        0,
        0,
        tiled=True,
        axis_index_groups=rings(),
    ).reshape(BLOCK, BLOCK)
    taps = jnp.concatenate([short_taps.reshape(9, 64), skip_gain[None]], axis=0)
    taps = lax.dynamic_slice_in_dim(taps, position * 8, 8, axis=1).T
    place, taps = lax.optimization_barrier((place, taps))

    weight = pl.pallas_call(
        weight_kernel,
        out_shape=jax.ShapeDtypeStruct((RING, 192, BLOCK), BF16),
        in_specs=[smem(), vmem()],
        out_specs=vmem(),
        compiler_params=params(12),
        cost_estimate=pl.CostEstimate(flops=0, bytes_accessed=3 << 20, transcendentals=0),
    )(place, in_weight.reshape(192, RING * BLOCK))
    two_a, two_b = shift(own, 2, -2), shift(own, -2, 2)
    before = pl.pallas_call(
        own_kernel,
        out_shape=jax.ShapeDtypeStruct((192, BLOCK), F32),
        in_specs=[smem(), vmem(), anywhere()],
        out_specs=vmem(),
        scratch_shapes=landing(1),
        compiler_params=params(12),
        cost_estimate=pl.CostEstimate(
            flops=2 * 192 * BLOCK * BLOCK, bytes_accessed=1 << 20, transcendentals=0
        ),
    )(place, weight, own)
    later, before = lax.optimization_barrier((own, before))
    one_a, one_b = shift(later, 1, -1), shift(later, -1, 1)
    four = shift(two_a, 2, -2)
    three_a, three_b = shift(two_a, 1, -1), shift(two_b, -1, 1)

    before = pl.pallas_call(
        first_kernel,
        out_shape=jax.ShapeDtypeStruct((192, BLOCK), F32),
        in_specs=[smem(), vmem(), vmem()] + [anywhere()] * 5,
        out_specs=vmem(),
        scratch_shapes=landing(5),
        compiler_params=params(12),
        cost_estimate=pl.CostEstimate(
            flops=2 * 5 * 192 * BLOCK * BLOCK, bytes_accessed=5 << 20, transcendentals=0
        ),
    )(place, weight, before, one_a, one_b, two_a, two_b, four)
    messages = pl.pallas_call(
        second_kernel,
        out_shape=jax.ShapeDtypeStruct((RING * 32, BLOCK), BF16),
        in_specs=[smem(), vmem(), vmem()] + [anywhere()] * 2 + [vmem()],
        out_specs=vmem(),
        scratch_shapes=landing(2),
        compiler_params=params(12),
        cost_estimate=pl.CostEstimate(
            flops=2 * 2 * 192 * BLOCK * BLOCK, bytes_accessed=3 << 20, transcendentals=0
        ),
    )(place, weight, before, three_a, three_b, long_filter)

    rows = lax.all_to_all(messages.reshape(RING, 32, BLOCK), "seq", 0, 0, tiled=True)
    forward, inverse = tables()
    mixed = pl.pallas_call(
        conv_kernel,
        out_shape=jax.ShapeDtypeStruct((RING * 8, BLOCK), BF16),
        in_specs=[vmem()] * 4,
        out_specs=vmem(),
        compiler_params=params(12),
        cost_estimate=pl.CostEstimate(
            flops=2 * (128 * 512 * 1024 + 64 * 1024 * 512), bytes_accessed=3 << 20, transcendentals=0
        ),
    )(rows.reshape(RING * 32, BLOCK), taps, forward, inverse)
    back = lax.all_to_all(mixed.reshape(RING, 8, BLOCK), "seq", 0, 0, tiled=True)
    return back.reshape(64, BLOCK).T


def solution(mesh):
    in_specs = (
        P("seq", "chan"),
        P(None, "chan", None),
        P(None, None, "chan"),
        P("chan", "seq"),
        P("chan"),
    )
    return jax.shard_map(
        on_device, mesh=mesh, in_specs=in_specs, out_specs=P("seq", "chan"), check_vma=False
    )
```

```python
import math

import jax
import jax.numpy as jnp
import numpy as np
from jax import lax
from jax.experimental import pallas as pl
from jax.experimental.pallas import tpu as pltpu
from jax.sharding import PartitionSpec as P

BOTH = ("seq", "chan")
RING = 8
BLOCK = 512
F32 = jnp.float32
BF16 = jnp.bfloat16


def device_number(x, core, z, y):
    return ((x * 2 + core) * RING + z % RING) * RING + y % RING


def devices():
    return [
        (x, core, z, y)
        for x in range(4)
        for core in range(2)
        for z in range(RING)
        for y in range(RING)
    ]


def rings():
    return [
        [
            device_number(x, core, line, i) if core == 1 else device_number(x, core, i, line)
            for i in range(RING)
        ]
        for x in range(4)
        for core in range(2)
        for line in range(RING)
    ]


def shift(block, even, odd):
    route = []
    for x, core, z, y in devices():
        here = z if core else y
        there = here + (odd if (here + 1) % 2 else even)
        route.append(
            (
                device_number(x, core, z, y),
                device_number(x, core, there, y) if core else device_number(x, core, z, there),
            )
        )
    return lax.ppermute(block, BOTH, route)


def tables():
    double = 2 * BLOCK
    freq = np.arange(BLOCK, dtype=np.int64)
    index = (freq[:, None] * freq[None, :]) % double
    phase = index.astype(np.float32) * np.float32(2.0 * math.pi / double)
    cosine = np.cos(phase).astype(jnp.bfloat16).astype(np.float32)
    sine = np.sin(phase).astype(jnp.bfloat16).astype(np.float32)
    nyquist = (1 - 2 * (freq % 2)).astype(np.float32)
    real, imag = cosine, -sine
    imag = imag.copy()
    imag[0] = nyquist
    forward = np.concatenate([real.T, imag.T], axis=1)
    weight = np.full((BLOCK, 1), 2.0 / double, np.float32)
    weight[0] = 1.0 / double
    inverse = np.concatenate([real * weight, imag * weight], axis=0)
    return forward.astype(jnp.bfloat16), inverse.astype(jnp.bfloat16)


def vmem():
    return pl.BlockSpec(memory_space=pltpu.VMEM)


def smem():
    return pl.BlockSpec(memory_space=pltpu.SMEM)


def anywhere():
    return pl.BlockSpec(memory_space=pl.ANY)


def landing(count):
    return [pltpu.VMEM((count, BLOCK, BLOCK), BF16), pltpu.SemaphoreType.DMA((count,))]


def params(mib):
    return pltpu.CompilerParams(vmem_limit_bytes=mib * 1024 * 1024)


def weight_kernel(place, weight, out):
    @pl.when(place[0] == 0)
    def _():
        for b in range(RING):
            out[b] = weight[:, b * BLOCK : (b + 1) * BLOCK]

    @pl.when(place[0] != 0)
    def _():
        for b in range(RING):
            out[b] = jnp.concatenate(
                [weight[:, (i * RING + b) * 64 : (i * RING + b) * 64 + 64] for i in range(RING)],
                axis=1,
            )


def project(place, weight, offsets, blocks, near, done, total):
    r = place[1]
    sign = 1 - 2 * lax.rem(r + 1, 2)
    copies = [
        pltpu.make_async_copy(block, near.at[i], done.at[i]) for i, block in enumerate(blocks)
    ]
    for copy in copies:
        copy.start()
    for i, offset in enumerate(offsets):
        copies[i].wait()
        part = jnp.dot(
            weight[lax.rem(r + sign * offset + RING, RING)],
            near[i],
            preferred_element_type=F32,
        )
        total = part if total is None else total + part
    return total


def own_kernel(place, weight, own, out, near, done):
    out[...] = project(place, weight, (0,), (own,), near, done, None)


def first_kernel(place, weight, before, one_a, one_b, two_a, two_b, four, out, near, done):
    blocks = (one_a, one_b, two_a, two_b, four)
    out[...] = project(place, weight, (1, -1, -2, 2, 4), blocks, near, done, before[...])


def second_kernel(place, weight, before, three_a, three_b, lags, out, near, done):
    total = project(place, weight, (3, -3), (three_a, three_b), near, done, before[...])
    lag_rows = lags[...].astype(F32)
    pieces = []
    for d in range(RING):
        for s in range(3):
            pieces.append(total[s * 64 + d * 8 : s * 64 + d * 8 + 8])
        pieces.append(lag_rows[d * 8 : d * 8 + 8])
    out[...] = jnp.concatenate(pieces, axis=0).astype(BF16)


def conv_kernel(rows, taps, forward, inverse, out):
    data = rows[...].astype(F32)
    lane = lax.broadcasted_iota(jnp.int32, (8, RING * BLOCK), 1)

    def stream(s):
        return jnp.concatenate(
            [data[b * 32 + s * 8 : b * 32 + s * 8 + 8] for b in range(RING)], axis=1
        )

    def feature(s):
        now = stream(s)
        one = jnp.where(lane < 1, 0.0, pltpu.roll(now, 1, 1))
        two = jnp.where(lane < 2, 0.0, pltpu.roll(now, 2, 1))
        t = [taps[:, s * 3 + j : s * 3 + j + 1] for j in range(3)]
        return t[0] * now + t[1] * one + t[2] * two

    def by_block(value):
        return jnp.concatenate(
            [value[:, b * BLOCK : (b + 1) * BLOCK] for b in range(RING)], axis=0
        )

    gated = by_block(feature(1) * feature(2)).astype(BF16)
    lags = jnp.concatenate([data[b * 32 + 24 : b * 32 + 32] for b in range(RING)], axis=0)
    spec = jnp.dot(
        jnp.concatenate([gated, lags.astype(BF16)], axis=0),
        forward[...],
        preferred_element_type=F32,
    )
    reals, imags = [[] for _ in range(RING)], [[] for _ in range(RING)]
    wide = 128
    for piece in range(BLOCK // wide):
        here = slice(piece * wide, (piece + 1) * wide)
        there = slice(BLOCK + piece * wide, BLOCK + (piece + 1) * wide)
        freq = lax.broadcasted_iota(jnp.int32, (8, wide), 1) + piece * wide
        sign = (1 - 2 * lax.rem(freq, 2)).astype(F32)
        sig_re = [spec[b * 8 : b * 8 + 8, here] for b in range(RING)]
        sig_im = [spec[b * 8 : b * 8 + 8, there] for b in range(RING)]
        fil_re, fil_im, fil_last = [], [], []
        for m in range(RING):
            row = 64 + m * 8
            re, im = spec[row : row + 8, here], spec[row : row + 8, there]
            if m:
                re = re + sign * spec[row - 8 : row, here]
                im = im + sign * spec[row - 8 : row, there]
            fil_re.append(re)
            if piece == 0:
                fil_im.append(jnp.where(freq == 0, 0.0, im))
                fil_last.append(jnp.where(freq == 0, im, re))
            else:
                fil_im.append(im)
                fil_last.append(re)
        for b in range(RING):
            re = im = None
            for j in range(b + 1):
                m = b - j
                one = fil_re[m] * sig_re[j] - fil_im[m] * sig_im[j]
                two = fil_last[m] * sig_im[j] + fil_im[m] * sig_re[j]
                re = one if re is None else re + one
                im = two if im is None else im + two
            reals[b].append(re)
            imags[b].append(im)
    product = jnp.concatenate(
        [jnp.concatenate(reals[b] + imags[b], axis=1) for b in range(RING)], axis=0
    ).astype(BF16)
    conv = jnp.dot(product, inverse[...], preferred_element_type=F32)
    query = by_block(feature(0))
    skip = jnp.concatenate([taps[:, 9:10]] * RING, axis=0)
    out[...] = (query * (conv + skip * gated.astype(F32))).astype(BF16)


def on_device(activations, in_weight, short_taps, long_filter, skip_gain):
    position = lax.axis_index("seq")
    mixed_blocks = 1 - position % 2
    chan = lax.axis_index("chan")
    ring_place = jnp.where(mixed_blocks == 0, chan // RING, chan % RING)
    place = jnp.stack([mixed_blocks, ring_place]).astype(jnp.int32)

    shard = activations.T
    own = lax.all_to_all(
        jnp.broadcast_to(shard[None], (RING,) + shard.shape),
        BOTH,
        0,
        0,
        tiled=True,
        axis_index_groups=rings(),
    ).reshape(BLOCK, BLOCK)
    taps = jnp.concatenate([short_taps.reshape(9, 64), skip_gain[None]], axis=0)
    taps = lax.dynamic_slice_in_dim(taps, position * 8, 8, axis=1).T
    place, taps = lax.optimization_barrier((place, taps))

    weight = pl.pallas_call(
        weight_kernel,
        out_shape=jax.ShapeDtypeStruct((RING, 192, BLOCK), BF16),
        in_specs=[smem(), vmem()],
        out_specs=vmem(),
        compiler_params=params(12),
        cost_estimate=pl.CostEstimate(flops=0, bytes_accessed=3 << 20, transcendentals=0),
    )(place, in_weight.reshape(192, RING * BLOCK))
    two_a, two_b = shift(own, 2, -2), shift(own, -2, 2)
    before = pl.pallas_call(
        own_kernel,
        out_shape=jax.ShapeDtypeStruct((192, BLOCK), F32),
        in_specs=[smem(), vmem(), anywhere()],
        out_specs=vmem(),
        scratch_shapes=landing(1),
        compiler_params=params(12),
        cost_estimate=pl.CostEstimate(
            flops=2 * 192 * BLOCK * BLOCK, bytes_accessed=1 << 20, transcendentals=0
        ),
    )(place, weight, own)
    later, before = lax.optimization_barrier((own, before))
    one_a, one_b = shift(later, 1, -1), shift(later, -1, 1)
    four = shift(two_a, 2, -2)
    three_a, three_b = shift(two_a, 1, -1), shift(two_b, -1, 1)

    before = pl.pallas_call(
        first_kernel,
        out_shape=jax.ShapeDtypeStruct((192, BLOCK), F32),
        in_specs=[smem(), vmem(), vmem()] + [anywhere()] * 5,
        out_specs=vmem(),
        scratch_shapes=landing(5),
        compiler_params=params(12),
        cost_estimate=pl.CostEstimate(
            flops=2 * 5 * 192 * BLOCK * BLOCK, bytes_accessed=5 << 20, transcendentals=0
        ),
    )(place, weight, before, one_a, one_b, two_a, two_b, four)
    messages = pl.pallas_call(
        second_kernel,
        out_shape=jax.ShapeDtypeStruct((RING * 32, BLOCK), BF16),
        in_specs=[smem(), vmem(), vmem()] + [anywhere()] * 2 + [vmem()],
        out_specs=vmem(),
        scratch_shapes=landing(2),
        compiler_params=params(12),
        cost_estimate=pl.CostEstimate(
            flops=2 * 2 * 192 * BLOCK * BLOCK, bytes_accessed=3 << 20, transcendentals=0
        ),
    )(place, weight, before, three_a, three_b, long_filter)

    rows = lax.all_to_all(messages.reshape(RING, 32, BLOCK), "seq", 0, 0, tiled=True)
    forward, inverse = tables()
    mixed = pl.pallas_call(
        conv_kernel,
        out_shape=jax.ShapeDtypeStruct((RING * 8, BLOCK), BF16),
        in_specs=[vmem()] * 4,
        out_specs=vmem(),
        compiler_params=params(12),
        cost_estimate=pl.CostEstimate(
            flops=2 * (128 * 512 * 1024 + 64 * 1024 * 512), bytes_accessed=3 << 20, transcendentals=0
        ),
    )(rows.reshape(RING * 32, BLOCK), taps, forward, inverse)
    back = lax.all_to_all(mixed.reshape(RING, 8, BLOCK), "seq", 0, 0, tiled=True)
    return back.reshape(64, BLOCK).T


def solution(mesh):
    in_specs = (
        P("seq", "chan"),
        P(None, "chan", None),
        P(None, None, "chan"),
        P("chan", "seq"),
        P("chan"),
    )
    return jax.shard_map(
        on_device, mesh=mesh, in_specs=in_specs, out_specs=P("seq", "chan"), check_vma=False
    )
```
